256 devices in a mesh: row: 8 (over x_lo, y), col: 32 (over z, x_hi, core).
Axes of the slice: x: 4 (x_hi: 2, x_lo: 2; x = x_hi * 2 + x_lo), y: 4, z: 8, core: 2. Of those that a mesh axis runs over, the one named last changes fastest.
Arguments:
- row_emb: float32 [32, 512, 256], P('row', 'col'), may hold values from -1.8 to 1.8
- col_emb: float32 [128, 512, 256], P('col', 'row'), may hold values from -1.8 to 1.8
- row_marg: bfloat16 [32, 512], P('row', 'col'), may hold values from 0.5 to 3
- col_marg: bfloat16 [128, 512], P('col', 'row'), may hold values from 0.5 to 3
- tile_list: int32 [8, 32, 8, 2], P('row', 'col'), may hold values from 0 to 127, as said below
- tile_count: int32 [8, 32], P('row', 'col'), may hold values from 1 to 8, as said below
- tile_data: int32 [8, 32, 8, 512, 512], P('row', 'col'), may hold values from 0 to 215
Outputs:
- row_new: float32 [32, 512, 256], P('row', 'col')
- col_new: float32 [128, 512, 256], P('col', 'row')
The draws below stay inside these ranges and needn't reach their ends.
Inputs may be any that keep to these rules, and one draw needn't show every extreme that they name: `tile_list`: the slots of device (r, c) name distinct tiles with row block in r * 4 to (r + 1) * 4 - 1 and column block in c * 4 to (c + 1) * 4 - 1; slots at or past the device's tile_count are not used. `tile_count`: some device uses all 8 slots.
All inputs are finite; a program needn't handle non-finite values.
Results may differ from the reference program's by a relative error of at most 0.012.
Values may be sent and summed in bfloat16 or wider, within the bound.
A program may use at most 64 MiB of HBM per device.

```python
import jax
import jax.numpy as jnp
from jax import lax

K = 256
B = 512
RB_DEV = 4
CB_DEV = 4
SLOTS = 8
NRB = 32
NCB = 128


def tile_plan(key):
    base = jax.random.fold_in(key, 7)
    n_row = NRB // RB_DEV
    n_col = NCB // CB_DEV
    devices = n_row * n_col
    keys = jax.random.split(base, devices)
    orders = jax.vmap(lambda k: jax.random.permutation(k, RB_DEV * CB_DEV))(keys)[:, :SLOTS]
    device_ids = jnp.arange(devices, dtype=jnp.int32)
    row_start = device_ids // n_col * RB_DEV
    col_start = device_ids % n_col * CB_DEV
    global_rows = row_start[:, None] + orders // CB_DEV
    global_cols = col_start[:, None] + orders % CB_DEV
    listing = jnp.stack([global_rows, global_cols], -1).astype(jnp.int32).reshape(n_row, n_col, SLOTS, 2)
    first = jax.random.randint(jax.random.fold_in(base, 1), (devices,), 1, SLOTS + 1)
    second = jax.random.randint(jax.random.fold_in(base, 2), (devices,), 1, SLOTS + 1)
    loads = jnp.maximum(first * second // SLOTS, 1)
    busiest = jax.random.randint(jax.random.fold_in(base, 3), (), 0, devices)
    loads = jnp.where(device_ids == busiest, SLOTS, loads).astype(jnp.int32).reshape(n_row, n_col)
    return (listing, loads)


def draw_tile_list(key, part):
    return tile_plan(key)[0]


def draw_tile_count(key, part):
    return tile_plan(key)[1]


def draw_tile_data(key, part):
    n_row = NRB // RB_DEV
    n_col = NCB // CB_DEV
    raw = jax.random.randint(jax.random.fold_in(key, 11), (n_row, n_col, SLOTS, B, B), 0, 1024)
    return jnp.maximum(raw * raw // 4096 - 40, 0).astype(jnp.int32)


def levels(key, dims, cuts, smallest, high):
    factor_of, own = 1.0, jax.random.fold_in(key, 6)
    for axis_at, shards_of in cuts:
        draws = jnp.exp(jax.random.uniform(jax.random.fold_in(own, axis_at), (shards_of,), jnp.float32, smallest / len(cuts), high / len(cuts)))
        factor_of = factor_of * jnp.repeat(draws, dims[axis_at] // shards_of).reshape([-1 if axis == axis_at else 1 for axis in range(len(dims))])
    return factor_of


def normal_values(stream_key, extent, scale, most, cuts=(), held_as=jnp.bfloat16):
    loudness = levels(stream_key, extent, cuts, -0.22, 0.18) if cuts else 1.0
    result = jax.random.normal(stream_key, extent, jnp.float32) * scale * loudness
    return jnp.minimum(jnp.maximum(result, -most), most).astype(held_as)


def setup_inputs(seed: int = 0) -> dict:
    key_list = jax.random.split(jax.random.key(seed), 8)
    return {
        "row_emb": normal_values(key_list[0], (NRB, B, K), 0.3, 1.8, ((0, 8), (1, 32)), jnp.float32),
        "col_emb": normal_values(key_list[1], (NCB, B, K), 0.3, 1.8, ((0, 32), (1, 8)), jnp.float32),
        "row_marg": jnp.clip(0.5 + 2.5 * jax.random.uniform(key_list[2], (NRB, B), jnp.float32) ** levels(key_list[2], (NRB, B), ((0, 8), (1, 32)), -0.2, 0.2), 0.5, 3.0).astype(jnp.bfloat16),
        "col_marg": jnp.clip(0.5 + 2.5 * jax.random.uniform(key_list[3], (NCB, B), jnp.float32) ** levels(key_list[3], (NCB, B), ((0, 32), (1, 8)), -0.2, 0.2), 0.5, 3.0).astype(jnp.bfloat16),
        "tile_list": draw_tile_list(jax.random.fold_in(key_list[7], 71), 0),
        "tile_count": draw_tile_count(jax.random.fold_in(key_list[7], 71), 0),
        "tile_data": draw_tile_data(jax.random.fold_in(key_list[7], 71), 0),
    }


def tile_signal(scores, counts, marg_left, marg_right):
    level = counts.astype(jnp.float32)
    diff = scores - (jnp.log(jnp.maximum(level, 1.0)) - marg_left[:, None] - marg_right[None, :])
    weight = 0.1 + 0.25 * jnp.sqrt(level)
    return jnp.where(level > 0.0, weight * diff, jax.nn.sigmoid(diff))

def substep(row_emb, col_emb, row_marg, col_marg, tile_list, tile_count, tile_data):
    row_panel = row_emb.astype(jnp.bfloat16)
    col_panel = col_emb.astype(jnp.bfloat16)
    row_margf = row_marg.astype(jnp.float32)
    col_margf = col_marg.astype(jnp.float32)
    flat_list = tile_list.reshape(-1, 2)
    flat_data = tile_data.reshape(-1, B, B)
    slot_ids = jnp.arange(SLOTS, dtype=jnp.int32)
    usable = (slot_ids[None, None, :] < tile_count[:, :, None]).reshape(-1)

    def one_tile(carry, item):
        grad_row, grad_col = carry
        pair, counts, valid = item
        i = pair[0].astype(jnp.int32)
        j = pair[1].astype(jnp.int32)
        row_piece = lax.dynamic_index_in_dim(row_panel, i, 0, keepdims=False)
        col_piece = lax.dynamic_index_in_dim(col_panel, j, 0, keepdims=False)
        scores = lax.dot_general(row_piece, col_piece, (((1,), (1,)), ((), ())), preferred_element_type=jnp.float32)
        marg_left = lax.dynamic_index_in_dim(row_margf, i, 0, keepdims=False)
        marg_right = lax.dynamic_index_in_dim(col_margf, j, 0, keepdims=False)
        signal = tile_signal(scores, counts, marg_left, marg_right).astype(jnp.bfloat16)
        row_term = jnp.dot(signal, col_piece, preferred_element_type=jnp.float32)
        col_term = lax.dot_general(signal, row_piece, (((0,), (0,)), ((), ())), preferred_element_type=jnp.float32)
        row_term = jnp.where(valid, row_term, jnp.zeros_like(row_term))
        col_term = jnp.where(valid, col_term, jnp.zeros_like(col_term))
        return ((grad_row.at[i].add(row_term), grad_col.at[j].add(col_term)), None)
    start = (jnp.zeros(row_emb.shape, jnp.float32), jnp.zeros(col_emb.shape, jnp.float32))
    (grad_row, grad_col), _ = lax.scan(one_tile, start, (flat_list, flat_data, usable))
    return (row_emb - 0.0004 * grad_row, col_emb - 0.0004 * grad_col)

def reference(row_emb, col_emb, row_marg, col_marg, tile_list, tile_count, tile_data):
    for substep_index in range(2):
        row_emb, col_emb = substep(row_emb, col_emb, row_marg, col_marg, tile_list, tile_count, tile_data)
    return (row_emb, col_emb)
```

```python
import jax
import jax.numpy as jnp
from jax import lax
from jax.experimental import pallas as pl
from jax.experimental.pallas import tpu as pltpu
from jax.sharding import PartitionSpec as P

MESH = pl.DeviceIdType.MESH
BF16, F32 = jnp.bfloat16, jnp.float32
B, K = 512, 256
SLOTS = 8
NY = 4
NROW = 8
NZ = 8
NZX = 16
ROWS, COLS = 16, 64
CHUNK = 256


def place(q):
    n = q // 2
    odd = lax.rem(n, 2)
    dz = lax.rem(odd * ((n + 1) // 2) + (1 - odd) * (NZ - n // 2), NZ)
    return dz, lax.rem(q, 2)


def kernel(
    count_ref, list_ref, row_ref, col_ref, rowm_ref, colm_ref, data_ref, row_out, col_out,
    row_panel, col_panel, row_marg, col_marg, marg_left, marg_right, minus_log, weight,
    stage, row_term, col_term, row_send, row_half, row_sum, row_got, col_send, col_got, slot_of, pair_of,
    data_sem, rp_s, rp_r, rf_s, rf_r, cp_s, cp_r, rm_s, rm_r, rmf_s, rmf_r, cm_s, cm_r,
    sib_s, sib_r, rg_s, rg_r, cg_s, cg_r,
):
    r, c = lax.axis_index("row"), lax.axis_index("col")
    xl, y = r // NY, lax.rem(r, NY)
    zx, core = c // 2, lax.rem(c, 2)
    z, xh = zx // 2, lax.rem(zx, 2)
    sibling = {"row": r, "col": zx * 2 + (1 - core)}

    def to_zx(q):
        dz, dx = place(q)
        return lax.rem(z + dz, NZ) * 2 + lax.rem(xh + dx, 2)

    def from_zx(q):
        dz, dx = place(q)
        return lax.rem(z - dz + NZ, NZ) * 2 + lax.rem(xh + dx, 2)

    def zx_device(t):
        return {"row": r, "col": t * 2 + core}

    def to_row(q):
        return lax.rem(xl + q // NY, 2) * NY + lax.rem(y + lax.rem(q, NY), NY)

    def from_row(q):
        return lax.rem(xl + q // NY, 2) * NY + lax.rem(y - lax.rem(q, NY) + NY, NY)

    def row_device(t):
        return {"row": t, "col": c}

    def copy(src, dst, send, recv, device):
        return pltpu.make_async_remote_copy(
            src_ref=src, dst_ref=dst, send_sem=send, recv_sem=recv, device_id=device, device_id_type=MESH
        )

    def loop(lo, hi, body):
        def step(i, carry):
            body(i)
            return carry

        lax.fori_loop(lo, hi, step, 0)

    barrier = pltpu.get_barrier_semaphore()

    def greet_zx(q):
        pl.semaphore_signal(barrier, inc=1, device_id=zx_device(to_zx(q)), device_id_type=MESH)

    def greet_row(q):
        pl.semaphore_signal(barrier, inc=1, device_id=row_device(to_row(q)), device_id_type=MESH)

    loop(1, NZX, greet_zx)
    loop(1, NROW, greet_row)
    pl.semaphore_signal(barrier, inc=1, device_id=sibling, device_id_type=MESH)

    def data_copy(s):
        return pltpu.make_async_copy(data_ref.at[0, 0, s], stage.at[s], data_sem.at[s])

    loop(0, SLOTS, lambda s: data_copy(s).start())

    row_out[...] = row_ref[...]
    col_out[...] = col_ref[...]
    row_marg[c] = rowm_ref[...]
    col_marg[r] = colm_ref[...]
    row_term[SLOTS] = jnp.zeros((B, K), F32)
    col_term[SLOTS] = jnp.zeros((B, K), F32)

    codes = []
    for s in range(SLOTS):
        i = jnp.clip(list_ref[s, 0] - r * 4, 0, 3)
        j = jnp.clip(list_ref[s, 1] - c * 4, 0, 3)
        pair_of[s, 0] = i
        pair_of[s, 1] = j
        codes.append(jnp.where(s < count_ref[0], i * 4 + j, -1))
    for pair in range(16):
        found = jnp.int32(SLOTS)
        for s in range(SLOTS):
            found = jnp.where(codes[s] == pair, s, found)
        slot_of[pair] = found

    def row_panel_send(p, q):
        mine = row_panel.at[p, c]
        return copy(mine, mine, rp_s.at[p, q], rp_r.at[p, q], zx_device(to_zx(q)))

    def row_panel_recv(p, q):
        t = from_zx(q)
        got = row_panel.at[p, t * 2 + core]
        return copy(got, got, rp_s.at[p, q], rp_r.at[p, q], zx_device(t))

    def row_panel_hand(p, q):
        got = row_panel.at[p, from_zx(q) * 2 + core]
        return copy(got, got, rf_s.at[p, q], rf_r.at[p, q], sibling)

    def row_panel_handed(p, q):
        got = row_panel.at[p, from_zx(q) * 2 + (1 - core)]
        return copy(got, got, rf_s.at[p, q], rf_r.at[p, q], sibling)

    def col_panel_send(p, q):
        mine = col_panel.at[p, r]
        return copy(mine, mine, cp_s.at[p, q], cp_r.at[p, q], row_device(to_row(q)))

    def col_panel_recv(p, q):
        t = from_row(q)
        got = col_panel.at[p, t]
        return copy(got, got, cp_s.at[p, q], cp_r.at[p, q], row_device(t))

    def col_panel_pass(p, q):
        got = col_panel.at[p, (1 - xl) * NY + y]
        return copy(got, got, cp_s.at[p, q], cp_r.at[p, q], row_device(to_row(q - NY)))

    def row_marg_send(q):
        mine = row_marg.at[c]
        return copy(mine, mine, rm_s.at[q], rm_r.at[q], zx_device(to_zx(q)))

    def row_marg_recv(q):
        t = from_zx(q)
        got = row_marg.at[t * 2 + core]
        return copy(got, got, rm_s.at[q], rm_r.at[q], zx_device(t))

    def col_marg_send(q):
        mine = col_marg.at[r]
        return copy(mine, mine, cm_s.at[q], cm_r.at[q], row_device(to_row(q)))

    def col_marg_recv(q):
        t = from_row(q)
        got = col_marg.at[t]
        return copy(got, got, cm_s.at[q], cm_r.at[q], row_device(t))

    def gather_start(p):
        col_panel[p, r] = col_out[...].astype(BF16)
        row_panel[p, c] = row_out[...].astype(BF16)

    def row_gather_send(p):
        loop(1, NZX, lambda q: row_panel_send(p, NZX - q).start())
        row_panel_hand(p, 0).start()

    def col_gather_send(p):
        col_panel_send(p, NY).start()
        loop(1, NY, lambda q: col_panel_send(p, q).start())

    def hand_on(p, q):
        row_panel_recv(p, q).wait_recv()
        row_panel_hand(p, q).start()

    def pass_on(p):
        col_panel_recv(p, NY).wait_recv()
        loop(NY + 1, NROW, lambda q: col_panel_pass(p, q).start())

    def gather_end(p):
        loop(1, NY, lambda q: col_panel_recv(p, q).wait_recv())
        loop(NY + 1, NROW, lambda q: col_panel_recv(p, q).wait_recv())
        loop(0, NZX, lambda q: row_panel_handed(p, q).wait_recv())

    def gather_sent(p):
        loop(1, NZX, lambda q: row_panel_send(p, q).wait_send())
        loop(0, NZX, lambda q: row_panel_hand(p, q).wait_send())
        loop(1, NROW, lambda q: col_panel_send(p, q).wait_send())

    gather_start(0)
    pl.semaphore_wait(barrier, NZX - 1 + NROW - 1 + 1)
    col_gather_send(0)
    row_gather_send(0)
    loop(1, NROW, lambda q: col_marg_send(q).start())
    loop(1, NZX, lambda q: row_marg_send(q).start())

    def prepare(s):
        data_copy(s).wait()

        def part(h, carry):
            rows = pl.ds(pl.multiple_of(h * 64, 64), 64)
            level = stage[s, rows].astype(F32)
            minus_log[s, rows] = -jnp.log(jnp.maximum(level, 1.0)).astype(BF16)
            weight[s, rows] = jnp.where(level > 0.0, 0.1 + 0.25 * jnp.sqrt(level), 0.0).astype(BF16)
            return carry

        lax.fori_loop(0, B // 64, part, 0)

    def prepare_and_hand(s):
        prepare(s)
        hand_on(0, 2 * s + 1)

        @pl.when(s < SLOTS - 1)
        def _():
            hand_on(0, 2 * s + 2)

    loop(0, 3, prepare_and_hand)
    pass_on(0)
    loop(3, SLOTS, prepare_and_hand)

    loop(1, NROW, lambda q: col_marg_recv(q).wait_recv())
    loop(1, NZX, lambda q: row_marg_recv(q).wait_recv())

    def marg_pass(q):
        got = row_marg.at[from_zx(q) * 2 + core]
        return copy(got, got, rmf_s.at[q], rmf_r.at[q], sibling)

    def marg_passed(q):
        got = row_marg.at[from_zx(q) * 2 + (1 - core)]
        return copy(got, got, rmf_s.at[q], rmf_r.at[q], sibling)

    loop(0, NZX, lambda q: marg_pass(q).start())
    loop(0, NZX, lambda q: marg_passed(q).wait_recv())

    gather_end(0)
    spread = row_marg[...].reshape(B, 128)
    lane = lax.broadcasted_iota(jnp.int32, (B, 128), 1)
    place_in = lax.rem(lax.broadcasted_iota(jnp.int32, (B, 128), 0), ROWS)
    ones = jnp.ones((128, 128), BF16)
    for i in range(4):
        picked = jnp.where(lane == i * ROWS + place_in, spread.astype(F32), 0.0).astype(BF16)
        marg_left[i] = jnp.dot(picked, ones, preferred_element_type=F32)
    low = lax.broadcasted_iota(jnp.int32, (16, 128), 1) < COLS
    for g in range(NROW // 2):
        marg_right[:, g * 128 : (g + 1) * 128] = jnp.where(
            low, col_marg[2 * g].astype(F32), col_marg[2 * g + 1].astype(F32)
        )

    def tiles(p):
        def tile(s):
            i, j = pair_of[s, 0], pair_of[s, 1]
            col_piece = col_panel[p, :, j].reshape(B, K)
            row_piece = row_panel[p, :, i].reshape(B, K)
            right = marg_right[pl.ds(j, 1), :]
            total = None
            for h in range(B // CHUNK):
                rows = slice(h * CHUNK, (h + 1) * CHUNK)
                mine = row_piece[rows]
                left = marg_left[i, rows, :]
                scores = lax.dot_general(mine, col_piece, (((1,), (1,)), ((), ())), preferred_element_type=F32)
                left = jnp.concatenate([left] * (B // 128), axis=1)
                diff = scores + (minus_log[s, rows].astype(F32) + right) + left
                scale = weight[s, rows].astype(F32)
                signal = jnp.where(scale > 0.0, scale * diff, 0.5 * jnp.tanh(0.5 * diff) + 0.5).astype(BF16)
                row_term[s, rows] = jnp.dot(signal, col_piece, preferred_element_type=F32)
                part = lax.dot_general(signal, mine, (((0,), (0,)), ((), ())), preferred_element_type=F32)
                total = part if total is None else total + part
            col_term[s] = total

        loop(0, SLOTS, tile)

    def sibling_send(p):
        return copy(row_send.at[1 - core], row_half.at[p], sib_s.at[p], sib_r.at[p], sibling)

    def row_grad_send(p, q):
        t = to_zx(q)
        return copy(row_sum.at[t], row_got.at[p, q], rg_s.at[p, q], rg_r.at[p, q], zx_device(t))

    def col_grad_send(p, q):
        t = to_row(q)
        return copy(col_send.at[t], col_got.at[p, q], cg_s.at[p, q], cg_r.at[p, q], row_device(t))

    def scatter_start(p):
        def row_part(t):
            for k in range(2):
                rows = pl.ds(pl.multiple_of(t * 32 + k * ROWS, ROWS), ROWS)
                for i in range(4):
                    found = [row_term[slot_of[i * 4 + j], rows, :] for j in range(4)]
                    row_send[k, t, i] = ((found[0] + found[1]) + (found[2] + found[3])).astype(BF16)

        loop(0, NZX, row_part)
        sibling_send(p).start()

        def col_part(t):
            for part in range(2):
                rows = pl.ds(pl.multiple_of(t * COLS + part * 32, 32), 32)
                for j in range(4):
                    found = [col_term[slot_of[i * 4 + j], rows, :] for i in range(4)]
                    col_send[t, j, part * 32 : part * 32 + 32] = (
                        (found[0] + found[1]) + (found[2] + found[3])
                    ).astype(BF16)

        loop(0, NROW, col_part)
        loop(1, NROW, lambda q: col_grad_send(p, NROW - q).start())
        sibling_send(p).wait_recv()

        def add(t):
            row_sum[t] = (row_send[core, t].astype(F32) + row_half[p, t].astype(F32)).astype(BF16)

        loop(0, NZX, add)
        loop(1, NZX, lambda q: row_grad_send(p, NZX - q).start())

    def col_update(p):
        loop(1, NROW, lambda q: col_grad_send(p, q).wait_recv())
        for j in range(4):
            total = col_send[r, j].astype(F32)
            for q in range(1, NROW):
                total = total + col_got[p, q, j].astype(F32)
            col_out[j] = col_out[j] - 0.0004 * total

    def row_update(p):
        loop(1, NZX, lambda q: row_grad_send(p, q).wait_recv())
        total = row_sum[zx].astype(F32)
        for q in range(1, NZX):
            total = total + row_got[p, q].astype(F32)
        row_out[...] = row_out[...] - 0.0004 * total

    def scatter_sent(p):
        loop(1, NROW, lambda q: col_grad_send(p, q).wait_send())
        loop(1, NZX, lambda q: row_grad_send(p, q).wait_send())
        sibling_send(p).wait_send()

    tiles(0)
    scatter_start(0)
    col_update(0)
    col_panel[1, r] = col_out[...].astype(BF16)
    col_gather_send(1)
    row_update(0)
    row_panel[1, c] = row_out[...].astype(BF16)
    row_gather_send(1)
    pass_on(1)
    loop(1, NZX, lambda q: hand_on(1, q))
    scatter_sent(0)
    gather_end(1)
    tiles(1)
    scatter_start(1)
    col_update(1)
    row_update(1)
    scatter_sent(1)
    gather_sent(0)
    gather_sent(1)
    loop(1, NROW, lambda q: col_marg_send(q).wait_send())
    loop(1, NZX, lambda q: row_marg_send(q).wait_send())
    loop(0, NZX, lambda q: marg_pass(q).wait_send())


def shards(row_emb, col_emb, row_marg, col_marg, tile_list, tile_count, tile_data):
    rowm = jnp.broadcast_to(jnp.pad(row_marg.reshape(1, 64), ((0, 0), (0, 64))), (16, 128))
    colm = jnp.tile(col_marg, (4, 2))
    vmem = pl.BlockSpec(memory_space=pltpu.VMEM)
    smem = pl.BlockSpec(memory_space=pltpu.SMEM)
    dma = pltpu.SemaphoreType.DMA
    return pl.pallas_call(
        kernel,
        out_shape=(
            jax.ShapeDtypeStruct(row_emb.shape, F32),
            jax.ShapeDtypeStruct(col_emb.shape, F32),
        ),
        in_specs=[smem, smem, vmem, vmem, vmem, vmem, pl.BlockSpec(memory_space=pl.ANY)],
        out_specs=(vmem, vmem),
        scratch_shapes=[
            pltpu.VMEM((2, 32, 4, ROWS, K), BF16),
            pltpu.VMEM((2, NROW, 4, COLS, K), BF16),
            pltpu.VMEM((32, 16, 128), BF16),
            pltpu.VMEM((NROW, 16, 128), BF16),
            pltpu.VMEM((4, B, 128), F32),
            pltpu.VMEM((16, B), F32),
            pltpu.VMEM((SLOTS, B, B), BF16),
            pltpu.VMEM((SLOTS, B, B), BF16),
            pltpu.VMEM((SLOTS, B, B), jnp.int32),
            pltpu.VMEM((SLOTS + 1, B, K), F32),
            pltpu.VMEM((SLOTS + 1, B, K), F32),
            pltpu.VMEM((2, NZX, 4, ROWS, K), BF16),
            pltpu.VMEM((2, NZX, 4, ROWS, K), BF16),
            pltpu.VMEM((NZX, 4, ROWS, K), BF16),
            pltpu.VMEM((2, NZX, 4, ROWS, K), BF16),
            pltpu.VMEM((NROW, 4, COLS, K), BF16),
            pltpu.VMEM((2, NROW, 4, COLS, K), BF16),
            pltpu.SMEM((16,), jnp.int32),
            pltpu.SMEM((SLOTS, 2), jnp.int32),
            dma((SLOTS,)),
            dma((2, NZX)), dma((2, NZX)), dma((2, NZX)), dma((2, NZX)),
            dma((2, NROW)), dma((2, NROW)),
            dma((NZX,)), dma((NZX,)), dma((NZX,)), dma((NZX,)), dma((NROW,)), dma((NROW,)),
            dma((2,)), dma((2,)),
            dma((2, NZX)), dma((2, NZX)), dma((2, NROW)), dma((2, NROW)),
        ],
        name="swivel",
        compiler_params=pltpu.CompilerParams(
            collective_id=0, has_side_effects=True, vmem_limit_bytes=60 * 2**20
        ),
        cost_estimate=pl.CostEstimate(flops=6_400_000_000, bytes_accessed=9_000_000, transcendentals=8_000_000),
    )(tile_count.reshape(1), tile_list.reshape(SLOTS, 2), row_emb, col_emb, rowm, colm, tile_data)


def solution(mesh):
    placed = (
        P("row", "col", None),
        P("col", "row", None),
        P("row", "col"),
        P("col", "row"),
        P("row", "col", None, None),
        P("row", "col"),
        P("row", "col", None, None, None),
    )
    return jax.shard_map(
        shards,
        mesh=mesh,
        in_specs=placed,
        out_specs=(P("row", "col", None), P("col", "row", None)),
        check_vma=False,
    )
```

```python
import functools

import jax
import jax.numpy as jnp
from jax import lax
from jax.experimental import pallas as pl
from jax.experimental.pallas import tpu as pltpu
from jax.sharding import PartitionSpec as P

MESH = pl.DeviceIdType.MESH
BF16, F32 = jnp.bfloat16, jnp.float32
B, K = 512, 256
SLOTS = 8
NY = 4
NROW = 8
NZ = 8
NZX = 16
ROWS, COLS = 16, 64
NEAR = 5


def offset(n):
    odd = lax.rem(n, 2) if not isinstance(n, int) else n % 2
    return odd * ((n + 1) // 2) - (1 - odd) * (n // 2)


def kernel(
    count_ref, list_ref, row_ref, col_ref, rowm_ref, colm_ref, data_ref, row_out, col_out,
    row_got_panel, col_panel, row_panel, tile_f32, picked, marg_left, marg_right, bias, weight,
    stage, row_term, col_term, row_send, row_half, row_sum, row_far, row_last, row_got,
    col_send, col_cross, col_got, slot_of, pair_of,
    data_sem, rp_s, rp_r, rf_s, rf_r, cp_s, cp_r,
    sib_s, sib_r, rg_s, rg_r, cg_s, cg_r,
):
    r, c = lax.axis_index("row"), lax.axis_index("col")
    xl, y = r // NY, lax.rem(r, NY)
    zx, core = c // 2, lax.rem(c, 2)
    z, xh = zx // 2, lax.rem(zx, 2)
    sibling = {"row": r, "col": zx * 2 + (1 - core)}
    across = (1 - xl) * NY + y

    def at_z(dz, other=0):
        side = xh if other == 0 else 1 - xh
        return {"row": r, "col": (lax.rem(z + dz + NZ, NZ) * 2 + side) * 2 + core}

    def at_y(dy):
        return {"row": xl * NY + lax.rem(y + dy, NY), "col": c}

    def at_x():
        return {"row": across, "col": c}

    def copy(src, dst, send, recv, device):
        return pltpu.make_async_remote_copy(
            src_ref=src, dst_ref=dst, send_sem=send, recv_sem=recv, device_id=device, device_id_type=MESH
        )

    def loop(lo, hi, body):
        def step(i, carry):
            body(i)
            return carry

        lax.fori_loop(lo, hi, step, 0)

    barrier = pltpu.get_barrier_semaphore()
    partners = [at_z(dz, other) for dz in (2, -2, 1, -1) for other in (0, 1)] + [at_z(0, 1)]
    partners += [at_y(dy) for dy in (2, 1, 3)] + [at_x(), sibling]
    for device in partners:
        pl.semaphore_signal(barrier, inc=1, device_id=device, device_id_type=MESH)

    def data_copy(s):
        return pltpu.make_async_copy(data_ref.at[0, 0, s], stage.at[s], data_sem.at[s])

    loop(0, SLOTS, lambda s: data_copy(s).start())

    row_out[...] = row_ref[...]
    col_out[...] = col_ref[...]
    tile_f32[...] = jnp.zeros((2, 16, K), F32)
    tile_f32[0, 0:4, 0:ROWS] = rowm_ref[...].astype(F32)
    tile_f32[1, 0:4, 0:COLS] = colm_ref[...].astype(F32)
    row_got_panel[0, core, 0, xh, 4] = tile_f32[0].astype(BF16)
    col_panel[0, r, 16] = tile_f32[1].astype(BF16)

    def pieces(p):
        return pl.ds(0, 5 if p == 0 else 4)

    def col_rows(p):
        return pl.ds(0, 17 if p == 0 else 16)

    def row_direct(p):
        mine = row_got_panel.at[p, core, 0, xh, pieces(p)]
        out = []
        for n in (3, 4, 1, 2, 0):
            for other in (0, 1):
                if n == 0 and other == 0:
                    continue
                sem = n * 2 + other
                there = row_got_panel.at[p, core, n, xh, pieces(p)]
                side = xh if other == 0 else 1 - xh
                here = row_got_panel.at[p, core, n, side, pieces(p)]
                device = at_z(offset(n), other)
                send = functools.partial(copy, mine, there, rp_s.at[p, sem], rp_r.at[p, sem], device)
                recv = functools.partial(copy, here, here, rp_s.at[p, sem], rp_r.at[p, sem], device)
                out.append((n, send, recv))
        return out

    def row_relay(p):
        out = []
        for sem, (src, dst, dz, side) in enumerate([(3, 5, 1, None), (4, 6, -1, None), (3, 7, 2, 0), (4, 7, -2, 1)]):
            at = pl.ds(0, 2) if side is None else pl.ds(side, 1)
            here = row_got_panel.at[p, core, src, at, pieces(p)]
            there = row_got_panel.at[p, core, dst, at, pieces(p)]
            out.append(copy(here, there, rp_s.at[p, 10 + sem], rp_r.at[p, 10 + sem], at_z(dz)))
        return out

    def row_hand(p, part, side):
        slots = pl.ds(0, NEAR) if part == 0 else pl.ds(NEAR, 8 - NEAR)
        block = row_got_panel.at[p, side, slots, :, pieces(p)]
        return copy(block, block, rf_s.at[p, part], rf_r.at[p, part], sibling)

    def col_direct(p, q):
        mine = col_panel.at[p, r, col_rows(p)]
        device = at_x() if q == NY else at_y(q)
        return copy(mine, mine, cp_s.at[p, q], cp_r.at[p, q], device)

    def col_direct_got(p, q):
        source = across if q == NY else xl * NY + lax.rem(y - q + NY, NY)
        got = col_panel.at[p, source, col_rows(p)]
        return copy(got, got, cp_s.at[p, q], cp_r.at[p, q], at_x())

    def col_pass(p, q):
        got = col_panel.at[p, across, col_rows(p)]
        return copy(got, got, cp_s.at[p, NY + q], cp_r.at[p, NY + q], at_y(q))

    def col_pass_got(p, q):
        source = (1 - xl) * NY + lax.rem(y - q + NY, NY)
        got = col_panel.at[p, source, col_rows(p)]
        return copy(got, got, cp_s.at[p, NY + q], cp_r.at[p, NY + q], at_x())

    ys = (2, 1, 3)

    def col_gather_send(p):
        for j in range(4):
            col_panel[p, r, 4 * j : 4 * j + 4] = col_out[j].astype(BF16).reshape(4, 16, K)
        col_direct(p, NY).start()
        for q in ys:
            col_direct(p, q).start()

    def row_gather_send(p):
        row_got_panel[p, core, 0, xh, 0:4] = row_out[...].astype(BF16)
        for _, send, _ in row_direct(p):
            send().start()

    def pass_on(p):
        col_direct_got(p, NY).wait_recv()
        for q in ys:
            col_pass(p, q).start()

    def relay(p):
        for n, _, recv in row_direct(p):
            if n in (3, 4):
                recv().wait_recv()
        for send in row_relay(p):
            send.start()

    def hand_near(p):
        for n, _, recv in row_direct(p):
            if n not in (3, 4):
                recv().wait_recv()
        row_hand(p, 0, core).start()

    def hand_far(p):
        for send in row_relay(p):
            send.wait_recv()
        row_hand(p, 1, core).start()

    def gather_end(p):
        for q in ys:
            col_direct_got(p, q).wait_recv()
        for q in ys:
            col_pass_got(p, q).wait_recv()
        for part in range(2):
            row_hand(p, part, 1 - core).wait_recv()

    def gather_sent(p):
        for _, send, _ in row_direct(p):
            send().wait_send()
        for send in row_relay(p):
            send.wait_send()
        for part in range(2):
            row_hand(p, part, core).wait_send()
        for q in (NY,) + ys:
            col_direct(p, q).wait_send()
        for q in ys:
            col_pass(p, q).wait_send()

    def arrange(p):
        def slot(n):
            source = lax.rem(z - offset(n) + 2 * NZ, NZ)
            for side in range(2):
                for k in range(2):
                    rows = pl.ds(pl.multiple_of(source * 64 + side * 32 + k * ROWS, ROWS), ROWS)
                    for i in range(4):
                        row_panel[i, rows, :] = row_got_panel[p, k, n, side, i]

        loop(0, 8, slot)

    pl.semaphore_wait(barrier, len(partners))
    col_gather_send(0)
    row_gather_send(0)

    row_term[SLOTS] = jnp.zeros((B, K), F32)
    col_term[SLOTS] = jnp.zeros((B, K), F32)
    codes = []
    for s in range(SLOTS):
        i = jnp.clip(list_ref[0, s] - r * 4, 0, 3)
        j = jnp.clip(list_ref[1, s] - c * 4, 0, 3)
        pair_of[s, 0] = i
        pair_of[s, 1] = j
        codes.append(jnp.where(s < count_ref[0, 0], i * 4 + j, -1))
    for pair in range(16):
        found = jnp.int32(SLOTS)
        for s in range(SLOTS):
            found = jnp.where(codes[s] == pair, s, found)
        slot_of[pair] = found

    def prepare(s):
        data_copy(s).wait()

        def part(h, carry):
            rows = pl.ds(pl.multiple_of(h * 64, 64), 64)
            level = stage[s, rows].astype(F32)
            bias[s, rows] = -jnp.log(jnp.maximum(level, 1.0)).astype(BF16)
            weight[s, rows] = jnp.where(level > 0.0, 0.1 + 0.25 * jnp.sqrt(level), 0.0).astype(BF16)
            return carry

        lax.fori_loop(0, B // 64, part, 0)

    loop(0, 4, prepare)
    pass_on(0)
    loop(4, 6, prepare)
    relay(0)
    hand_near(0)
    loop(6, SLOTS, prepare)
    hand_far(0)
    gather_end(0)
    arrange(0)

    lane = lax.broadcasted_iota(jnp.int32, (ROWS, 128), 1)
    mine = lane == lax.broadcasted_iota(jnp.int32, (ROWS, 128), 0)

    def pick(n):
        source = lax.rem(z - offset(n) + 2 * NZ, NZ)
        for side in range(2):
            for k in range(2):
                rows = pl.ds(pl.multiple_of(source * 64 + side * 32 + k * ROWS, ROWS), ROWS)
                margins = row_got_panel[0, k, n, side, 4].astype(F32)
                for i in range(4):
                    line = jnp.broadcast_to(margins[i : i + 1, 0:128], (ROWS, 128))
                    picked[i, rows, :] = jnp.where(mine, line, 0.0).astype(BF16)

    loop(0, 8, pick)
    ones = jnp.ones((128, 128), BF16)
    for i in range(4):
        marg_left[i] = jnp.dot(picked[i], ones, preferred_element_type=F32)
    for g in range(NROW // 2):
        low = col_panel[0, 2 * g, 16].astype(F32)[:, 0:128]
        high = col_panel[0, 2 * g + 1, 16].astype(F32)[:, 0:128]
        marg_right[:, g * 128 : (g + 1) * 128] = jnp.where(lane < COLS, low, pltpu.roll(high, COLS, 1))

    def tiles(p):
        def tile(s):
            i, j = pair_of[s, 0], pair_of[s, 1]
            col_piece = col_panel[p, :, pl.ds(4 * j, 4)].reshape(B, K)
            row_piece = row_panel[i]
            scores = lax.dot_general(row_piece, col_piece, (((1,), (1,)), ((), ())), preferred_element_type=F32)
            if p == 0:
                left = jnp.concatenate([marg_left[i]] * (B // 128), axis=1)
                shift = (bias[s].astype(F32) + marg_right[pl.ds(j, 1), :] + left).astype(BF16)
                bias[s] = shift
            else:
                shift = bias[s]
            diff = scores.astype(BF16) + shift
            scale = weight[s]
            signal = jnp.where(scale > 0, scale * diff, 0.5 * jnp.tanh(0.5 * diff) + 0.5).astype(BF16)
            row_term[s] = jnp.dot(signal, col_piece, preferred_element_type=F32)
            col_term[s] = lax.dot_general(signal, row_piece, (((0,), (0,)), ((), ())), preferred_element_type=F32)

        loop(0, SLOTS, tile)

    far, near = pl.ds(NEAR, 8 - NEAR), pl.ds(0, NEAR)

    def sibling_send(p, part):
        slots = near if part == 0 else far
        return copy(
            row_send.at[1 - core, slots], row_half.at[p, slots], sib_s.at[p, part], sib_r.at[p, part], sibling
        )

    def far_sends(p):
        return [
            copy(row_sum.at[5], row_far.at[p, 0], rg_s.at[p, 10], rg_r.at[p, 10], at_z(1)),
            copy(row_sum.at[6], row_far.at[p, 1], rg_s.at[p, 11], rg_r.at[p, 11], at_z(-1)),
            copy(row_sum.at[7, 0], row_last.at[p, 0], rg_s.at[p, 12], rg_r.at[p, 12], at_z(2)),
            copy(row_sum.at[7, 1], row_last.at[p, 1], rg_s.at[p, 13], rg_r.at[p, 13], at_z(-2)),
        ]

    def near_sends(p, slots):
        out = []
        for m in slots:
            for other in (0, 1):
                if m == 0 and other == 0:
                    continue
                sem = m * 2 + other
                side = xh if other == 0 else 1 - xh
                out.append(
                    copy(
                        row_sum.at[m, side], row_got.at[p, sem], rg_s.at[p, sem], rg_r.at[p, sem],
                        at_z(offset(m), other),
                    )
                )
        return out

    def cross_send(p, q):
        t = (1 - xl) * NY + lax.rem(y + q, NY)
        return copy(col_send.at[t], col_cross.at[p, q], cg_s.at[p, NY + q], cg_r.at[p, NY + q], at_y(q))

    def straight_send(p, q):
        t = xl * NY + lax.rem(y + q, NY)
        return copy(col_send.at[t], col_got.at[p, q], cg_s.at[p, q], cg_r.at[p, q], at_y(q))

    def across_send(p):
        return copy(col_send.at[across], col_got.at[p, 0], cg_s.at[p, NY], cg_r.at[p, NY], at_x())

    def row_part(m):
        dest = lax.rem(z + offset(m) + NZ, NZ)
        for side in range(2):
            for k in range(2):
                rows = pl.ds(pl.multiple_of(dest * 64 + side * 32 + k * ROWS, ROWS), ROWS)
                for i in range(4):
                    found = [row_term[slot_of[i * 4 + j], rows, :] for j in range(4)]
                    row_send[k, m, side, i] = ((found[0] + found[1]) + (found[2] + found[3])).astype(BF16)

    def col_part(t):
        for part in range(2):
            rows = pl.ds(pl.multiple_of(t * COLS + part * 32, 32), 32)
            for j in range(4):
                found = [col_term[slot_of[i * 4 + j], rows, :] for i in range(4)]
                col_send[t, j, part * 32 : part * 32 + 32] = (
                    (found[0] + found[1]) + (found[2] + found[3])
                ).astype(BF16)

    def add(p, m):
        for side in range(2):
            row_sum[m, side] = (
                row_send[core, m, side].astype(F32) + row_half[p, m, side].astype(F32)
            ).astype(BF16)

    def scatter(p):
        loop(NEAR, 8, row_part)
        sibling_send(p, 1).start()
        loop(0, NEAR, row_part)
        sibling_send(p, 0).start()
        loop(0, NY, lambda t: col_part((1 - xl) * NY + t))
        for q in ys:
            cross_send(p, q).start()
        sibling_send(p, 1).wait_recv()
        for m in range(NEAR, 8):
            add(p, m)
        for send in far_sends(p):
            send.start()
        loop(0, NY, lambda t: col_part(xl * NY + t))
        for q in ys:
            straight_send(p, q).start()
        sibling_send(p, 0).wait_recv()
        for m in range(NEAR):
            add(p, m)
        for send in near_sends(p, (1, 2, 0)):
            send.start()
        for send in far_sends(p):
            send.wait_recv()
        for m, e in ((3, 0), (4, 1)):
            for side in range(2):
                total = row_sum[m, side].astype(F32) + row_far[p, e, side].astype(F32)
                if side == e:
                    total = total + row_last[p, e].astype(F32)
                row_sum[m, side] = total.astype(BF16)
        for send in near_sends(p, (3, 4)):
            send.start()
        for q in ys:
            cross_send(p, q).wait_recv()
        for j in range(4):
            total = col_send[across, j].astype(F32)
            for q in ys:
                total = total + col_cross[p, q, j].astype(F32)
            col_send[across, j] = total.astype(BF16)
        across_send(p).start()

    def row_update(p):
        for send in near_sends(p, range(NEAR)):
            send.wait_recv()
        total = row_sum[0, xh].astype(F32)
        for sem in range(1, 2 * NEAR):
            total = total + row_got[p, sem].astype(F32)
        row_out[...] = row_out[...] - 0.0004 * total

    def col_update(p):
        for q in ys:
            straight_send(p, q).wait_recv()
        across_send(p).wait_recv()
        for j in range(4):
            total = col_send[r, j].astype(F32)
            for q in range(NY):
                total = total + col_got[p, q, j].astype(F32)
            col_out[j] = col_out[j] - 0.0004 * total

    def scatter_sent(p):
        for q in ys:
            cross_send(p, q).wait_send()
            straight_send(p, q).wait_send()
        across_send(p).wait_send()
        for send in far_sends(p) + near_sends(p, range(NEAR)):
            send.wait_send()
        for part in range(2):
            sibling_send(p, part).wait_send()

    tiles(0)
    scatter(0)
    row_update(0)
    row_gather_send(1)
    col_update(0)
    col_gather_send(1)
    scatter_sent(0)
    pass_on(1)
    relay(1)
    hand_near(1)
    hand_far(1)
    gather_end(1)
    arrange(1)
    tiles(1)
    scatter(1)
    row_update(1)
    col_update(1)
    scatter_sent(1)
    gather_sent(0)
    gather_sent(1)


def shards(row_emb, col_emb, row_marg, col_marg, tile_list, tile_count, tile_data):
    vmem = pl.BlockSpec(memory_space=pltpu.VMEM)
    smem = pl.BlockSpec(memory_space=pltpu.SMEM)
    dma = pltpu.SemaphoreType.DMA
    return pl.pallas_call(
        kernel,
        out_shape=(
            jax.ShapeDtypeStruct(row_emb.shape, F32),
            jax.ShapeDtypeStruct(col_emb.shape, F32),
        ),
        in_specs=[smem, smem, vmem, vmem, vmem, vmem, pl.BlockSpec(memory_space=pl.ANY)],
        out_specs=(vmem, vmem),
        scratch_shapes=[
            pltpu.VMEM((2, 2, 8, 2, 5, ROWS, K), BF16),
            pltpu.VMEM((2, NROW, 17, 16, K), BF16),
            pltpu.VMEM((4, B, K), BF16),
            pltpu.VMEM((2, 16, K), F32),
            pltpu.VMEM((4, B, 128), BF16),
            pltpu.VMEM((4, B, 128), F32),
            pltpu.VMEM((16, B), F32),
            pltpu.VMEM((SLOTS, B, B), BF16),
            pltpu.VMEM((SLOTS, B, B), BF16),
            pltpu.VMEM((SLOTS, B, B), jnp.int32),
            pltpu.VMEM((SLOTS + 1, B, K), F32),
            pltpu.VMEM((SLOTS + 1, B, K), F32),
            pltpu.VMEM((2, 8, 2, 4, ROWS, K), BF16),
            pltpu.VMEM((2, 8, 2, 4, ROWS, K), BF16),
            pltpu.VMEM((8, 2, 4, ROWS, K), BF16),
            pltpu.VMEM((2, 2, 2, 4, ROWS, K), BF16),
            pltpu.VMEM((2, 2, 4, ROWS, K), BF16),
            pltpu.VMEM((2, 2 * NEAR, 4, ROWS, K), BF16),
            pltpu.VMEM((NROW, 4, COLS, K), BF16),
            pltpu.VMEM((2, NY, 4, COLS, K), BF16),
            pltpu.VMEM((2, NY, 4, COLS, K), BF16),
            pltpu.SMEM((16,), jnp.int32),
            pltpu.SMEM((SLOTS, 2), jnp.int32),
            dma((SLOTS,)),
            dma((2, 14)), dma((2, 14)), dma((2, 2)), dma((2, 2)), dma((2, NROW)), dma((2, NROW)),
            dma((2, 2)), dma((2, 2)), dma((2, 14)), dma((2, 14)), dma((2, NROW)), dma((2, NROW)),
        ],
        name="swivel",
        compiler_params=pltpu.CompilerParams(
            collective_id=0, has_side_effects=True, vmem_limit_bytes=60 * 2**20
        ),
        cost_estimate=pl.CostEstimate(flops=6_400_000_000, bytes_accessed=9_000_000, transcendentals=8_000_000),
    )(tile_count, tile_list[0, 0].T, row_emb, col_emb, row_marg, col_marg, tile_data)


def solution(mesh):
    placed = (
        P("row", "col", None),
        P("col", "row", None),
        P("row", "col"),
        P("col", "row"),
        P("row", "col", None, None),
        P("row", "col"),
        P("row", "col", None, None, None),
    )
    return jax.shard_map(
        shards,
        mesh=mesh,
        in_specs=placed,
        out_specs=(P("row", "col", None), P("col", "row", None)),
        check_vma=False,
    )
```

```python
import functools

import jax
import jax.numpy as jnp
from jax import lax
from jax.experimental import pallas as pl
from jax.experimental.pallas import tpu as pltpu
from jax.sharding import PartitionSpec as P

MESH = pl.DeviceIdType.MESH
BF16, F32 = jnp.bfloat16, jnp.float32
B, K = 512, 256
SLOTS = 8
NY = 4
NROW = 8
NZ = 8
NZX = 16
ROWS, COLS = 16, 64
NEAR = 5


def offset(n):
    odd = lax.rem(n, 2) if not isinstance(n, int) else n % 2
    return odd * ((n + 1) // 2) - (1 - odd) * (n // 2)


def kernel(
    count_ref, list_ref, row_ref, col_ref, rowm_ref, colm_ref, data_ref, row_out, col_out, row_now, col_now,
    row_got_panel, col_panel, row_panel, tile_f32, picked, marg_left, marg_right, bias, weight,
    stage, row_term, col_term, row_send, row_half, row_sum, row_far, row_last, row_got,
    col_send, col_cross, col_got, slot_of, pair_of,
    data_sem, in_sem, out_sem, rp_s, rp_r, rf_s, rf_r, cp_s, cp_r,
    sib_s, sib_r, rg_s, rg_r, cg_s, cg_r,
):
    r, c = lax.axis_index("row"), lax.axis_index("col")
    xl, y = r // NY, lax.rem(r, NY)
    zx, core = c // 2, lax.rem(c, 2)
    z, xh = zx // 2, lax.rem(zx, 2)
    sibling = {"row": r, "col": zx * 2 + (1 - core)}
    across = (1 - xl) * NY + y

    def at_z(dz, other=0):
        side = xh if other == 0 else 1 - xh
        return {"row": r, "col": (lax.rem(z + dz + NZ, NZ) * 2 + side) * 2 + core}

    def at_y(dy):
        return {"row": xl * NY + lax.rem(y + dy, NY), "col": c}

    def at_x():
        return {"row": across, "col": c}

    def copy(src, dst, send, recv, device):
        return pltpu.make_async_remote_copy(
            src_ref=src, dst_ref=dst, send_sem=send, recv_sem=recv, device_id=device, device_id_type=MESH
        )

    def loop(lo, hi, body):
        def step(i, carry):
            body(i)
            return carry

        lax.fori_loop(lo, hi, step, 0)

    barrier = pltpu.get_barrier_semaphore()
    partners = [at_z(dz, other) for dz in (2, -2, 1, -1) for other in (0, 1)] + [at_z(0, 1)]
    partners += [at_y(dy) for dy in (2, 1, 3)] + [at_x(), sibling]
    for device in partners:
        pl.semaphore_signal(barrier, inc=1, device_id=device, device_id_type=MESH)

    def data_copy(s):
        return pltpu.make_async_copy(data_ref.at[0, 0, s], stage.at[s], data_sem.at[s])

    row_in = pltpu.make_async_copy(row_ref, row_now, in_sem.at[0])
    col_in = pltpu.make_async_copy(col_ref, col_now, in_sem.at[1])
    row_in.start()
    col_in.start()
    loop(0, SLOTS, lambda s: data_copy(s).start())

    tile_f32[...] = jnp.zeros((2, 16, K), F32)
    tile_f32[0, 0:4, 0:ROWS] = rowm_ref[...].astype(F32)
    tile_f32[1, 0:4, 0:COLS] = colm_ref[...].astype(F32)
    row_got_panel[0, core, 0, xh, 4] = tile_f32[0].astype(BF16)
    col_panel[0, r, 16] = tile_f32[1].astype(BF16)
    row_in.wait()
    col_in.wait()

    def pieces(p):
        return pl.ds(0, 5 if p == 0 else 4)

    def col_rows(p):
        return pl.ds(0, 17 if p == 0 else 16)

    def row_direct(p):
        mine = row_got_panel.at[p, core, 0, xh, pieces(p)]
        out = []
        for n in (3, 4, 1, 2, 0):
            for other in (0, 1):
                if n == 0 and other == 0:
                    continue
                sem = n * 2 + other
                there = row_got_panel.at[p, core, n, xh, pieces(p)]
                side = xh if other == 0 else 1 - xh
                here = row_got_panel.at[p, core, n, side, pieces(p)]
                device = at_z(offset(n), other)
                send = functools.partial(copy, mine, there, rp_s.at[p, sem], rp_r.at[p, sem], device)
                recv = functools.partial(copy, here, here, rp_s.at[p, sem], rp_r.at[p, sem], device)
                out.append((n, send, recv))
        return out

    def row_relay(p):
        out = []
        for sem, (src, dst, dz, side) in enumerate([(3, 5, 1, None), (4, 6, -1, None), (3, 7, 2, 0), (4, 7, -2, 1)]):
            at = pl.ds(0, 2) if side is None else pl.ds(side, 1)
            here = row_got_panel.at[p, core, src, at, pieces(p)]
            there = row_got_panel.at[p, core, dst, at, pieces(p)]
            out.append(copy(here, there, rp_s.at[p, 10 + sem], rp_r.at[p, 10 + sem], at_z(dz)))
        return out

    def row_hand(p, part, side):
        slots = pl.ds(0, NEAR) if part == 0 else pl.ds(NEAR, 8 - NEAR)
        block = row_got_panel.at[p, side, slots, :, pieces(p)]
        return copy(block, block, rf_s.at[p, part], rf_r.at[p, part], sibling)

    def col_direct(p, q):
        mine = col_panel.at[p, r, col_rows(p)]
        device = at_x() if q == NY else at_y(q)
        return copy(mine, mine, cp_s.at[p, q], cp_r.at[p, q], device)

    def col_direct_got(p, q):
        source = across if q == NY else xl * NY + lax.rem(y - q + NY, NY)
        got = col_panel.at[p, source, col_rows(p)]
        return copy(got, got, cp_s.at[p, q], cp_r.at[p, q], at_x())

    def col_pass(p, q):
        source = xl * NY + lax.rem(y + 2, NY) if q == 2 else across
        got = col_panel.at[p, source, col_rows(p)]
        return copy(got, got, cp_s.at[p, NY + q], cp_r.at[p, NY + q], at_x() if q == 2 else at_y(q))

    def col_pass_got(p, q):
        source = (1 - xl) * NY + lax.rem(y - q + NY, NY)
        got = col_panel.at[p, source, col_rows(p)]
        return copy(got, got, cp_s.at[p, NY + q], cp_r.at[p, NY + q], at_x())

    ys = (2, 1, 3)

    def col_gather_send(p):
        col_direct(p, NY).start()
        for q in ys:
            col_direct(p, q).start()

    def col_round(p):
        for j in range(4):
            col_panel[p, r, 4 * j : 4 * j + 4] = col_now[j].astype(BF16).reshape(4, 16, K)

    def row_round(p):
        row_got_panel[p, core, 0, xh, 0:4] = row_now[...].astype(BF16)

    def row_gather_send(p):
        for _, send, _ in row_direct(p):
            send().start()

    def pass_on(p):
        col_direct_got(p, NY).wait_recv()
        for q in (1, 3):
            col_pass(p, q).start()

    def pass_back(p):
        col_direct_got(p, 2).wait_recv()
        col_pass(p, 2).start()

    def relay(p):
        for n, _, recv in row_direct(p):
            if n in (3, 4):
                recv().wait_recv()
        for send in row_relay(p):
            send.start()

    def hand_near(p):
        for n, _, recv in row_direct(p):
            if n not in (3, 4):
                recv().wait_recv()
        row_hand(p, 0, core).start()

    def hand_far(p):
        for send in row_relay(p):
            send.wait_recv()
        row_hand(p, 1, core).start()

    def gather_end(p):
        for q in (1, 3):
            col_direct_got(p, q).wait_recv()
        for q in ys:
            col_pass_got(p, q).wait_recv()
        for part in range(2):
            row_hand(p, part, 1 - core).wait_recv()

    def gather_sent(p):
        for _, send, _ in row_direct(p):
            send().wait_send()
        for send in row_relay(p):
            send.wait_send()
        for part in range(2):
            row_hand(p, part, core).wait_send()
        for q in (NY,) + ys:
            col_direct(p, q).wait_send()
        for q in ys:
            col_pass(p, q).wait_send()

    def arrange(p):
        def slot(n):
            source = lax.rem(z - offset(n) + 2 * NZ, NZ)
            for side in range(2):
                for k in range(2):
                    rows = pl.ds(pl.multiple_of(source * 64 + side * 32 + k * ROWS, ROWS), ROWS)
                    for i in range(4):
                        row_panel[i, rows, :] = row_got_panel[p, k, n, side, i]

        loop(0, 8, slot)

    col_round(0)
    row_round(0)
    pl.semaphore_wait(barrier, len(partners))
    col_gather_send(0)
    row_gather_send(0)

    row_term[SLOTS] = jnp.zeros((B, K), F32)
    col_term[SLOTS] = jnp.zeros((B, K), F32)
    codes = []
    for s in range(SLOTS):
        i = jnp.clip(list_ref[0, s] - r * 4, 0, 3)
        j = jnp.clip(list_ref[1, s] - c * 4, 0, 3)
        pair_of[s, 0] = i
        pair_of[s, 1] = j
        codes.append(jnp.where(s < count_ref[0, 0], i * 4 + j, -1))
    for pair in range(16):
        found = jnp.int32(SLOTS)
        for s in range(SLOTS):
            found = jnp.where(codes[s] == pair, s, found)
        slot_of[pair] = found

    def prepare(s):
        data_copy(s).wait()

        def part(h, carry):
            rows = pl.ds(pl.multiple_of(h * 64, 64), 64)
            level = stage[s, rows].astype(F32)
            bias[s, rows] = -jnp.log(jnp.maximum(level, 1.0)).astype(BF16)
            weight[s, rows] = jnp.where(level > 0.0, 0.1 + 0.25 * jnp.sqrt(level), 0.0).astype(BF16)
            return carry

        lax.fori_loop(0, B // 64, part, 0)

    loop(0, 4, prepare)
    pass_on(0)
    prepare(4)
    pass_back(0)
    prepare(5)
    relay(0)
    hand_near(0)
    loop(6, SLOTS, prepare)
    hand_far(0)
    gather_end(0)
    arrange(0)

    lane = lax.broadcasted_iota(jnp.int32, (ROWS, 128), 1)
    mine = lane == lax.broadcasted_iota(jnp.int32, (ROWS, 128), 0)

    def pick(n):
        source = lax.rem(z - offset(n) + 2 * NZ, NZ)
        for side in range(2):
            for k in range(2):
                rows = pl.ds(pl.multiple_of(source * 64 + side * 32 + k * ROWS, ROWS), ROWS)
                margins = row_got_panel[0, k, n, side, 4].astype(F32)
                for i in range(4):
                    line = jnp.broadcast_to(margins[i : i + 1, 0:128], (ROWS, 128))
                    picked[i, rows, :] = jnp.where(mine, line, 0.0).astype(BF16)

    loop(0, 8, pick)
    ones = jnp.ones((128, 128), BF16)
    for i in range(4):
        marg_left[i] = jnp.dot(picked[i], ones, preferred_element_type=F32)
    for g in range(NROW // 2):
        low = col_panel[0, 2 * g, 16].astype(F32)[:, 0:128]
        high = col_panel[0, 2 * g + 1, 16].astype(F32)[:, 0:128]
        marg_right[:, g * 128 : (g + 1) * 128] = jnp.where(lane < COLS, low, pltpu.roll(high, COLS, 1))

    def tiles(p):
        def tile(s):
            i, j = pair_of[s, 0], pair_of[s, 1]
            col_piece = col_panel[p, :, pl.ds(4 * j, 4)].reshape(B, K)
            row_piece = row_panel[i]
            scores = lax.dot_general(row_piece, col_piece, (((1,), (1,)), ((), ())), preferred_element_type=F32)
            if p == 0:
                left = jnp.concatenate([marg_left[i]] * (B // 128), axis=1)
                shift = (bias[s].astype(F32) + marg_right[pl.ds(j, 1), :] + left).astype(BF16)
                bias[s] = shift
            else:
                shift = bias[s]
            diff = scores.astype(BF16) + shift
            scale = weight[s]
            signal = jnp.where(scale > 0, scale * diff, 0.5 * jnp.tanh(0.5 * diff) + 0.5).astype(BF16)
            row_term[s] = jnp.dot(signal, col_piece, preferred_element_type=F32)
            col_term[s] = lax.dot_general(signal, row_piece, (((0,), (0,)), ((), ())), preferred_element_type=F32)

        for s in range(SLOTS):
            tile(s)

    far, near = pl.ds(NEAR, 8 - NEAR), pl.ds(0, NEAR)

    def sibling_send(p, part):
        slots = near if part == 0 else far
        return copy(
            row_send.at[1 - core, slots], row_half.at[p, slots], sib_s.at[p, part], sib_r.at[p, part], sibling
        )

    def far_sends(p):
        return [
            copy(row_sum.at[5], row_far.at[p, 0], rg_s.at[p, 10], rg_r.at[p, 10], at_z(1)),
            copy(row_sum.at[6], row_far.at[p, 1], rg_s.at[p, 11], rg_r.at[p, 11], at_z(-1)),
            copy(row_sum.at[7, 0], row_last.at[p, 0], rg_s.at[p, 12], rg_r.at[p, 12], at_z(2)),
            copy(row_sum.at[7, 1], row_last.at[p, 1], rg_s.at[p, 13], rg_r.at[p, 13], at_z(-2)),
        ]

    def near_sends(p, slots):
        out = []
        for m in slots:
            for other in (0, 1):
                if m == 0 and other == 0:
                    continue
                sem = m * 2 + other
                side = xh if other == 0 else 1 - xh
                out.append(
                    copy(
                        row_sum.at[m, side], row_got.at[p, sem], rg_s.at[p, sem], rg_r.at[p, sem],
                        at_z(offset(m), other),
                    )
                )
        return out

    def cross_send(p, q):
        t = (1 - xl) * NY + lax.rem(y + q, NY)
        device = at_x() if q == 2 else at_y(q)
        return copy(col_send.at[t], col_cross.at[p, q], cg_s.at[p, NY + q], cg_r.at[p, NY + q], device)

    def straight_send(p, q):
        t = xl * NY + lax.rem(y + q, NY)
        return copy(col_send.at[t], col_got.at[p, q], cg_s.at[p, q], cg_r.at[p, q], at_y(q))

    def across_send(p):
        return copy(col_send.at[across], col_got.at[p, 0], cg_s.at[p, NY], cg_r.at[p, NY], at_x())

    def row_part(m):
        dest = lax.rem(z + offset(m) + NZ, NZ)
        for side in range(2):
            for k in range(2):
                rows = pl.ds(pl.multiple_of(dest * 64 + side * 32 + k * ROWS, ROWS), ROWS)
                for i in range(4):
                    found = [row_term[slot_of[i * 4 + j], rows, :] for j in range(4)]
                    row_send[k, m, side, i] = ((found[0] + found[1]) + (found[2] + found[3])).astype(BF16)

    def col_part(t):
        for part in range(2):
            rows = pl.ds(pl.multiple_of(t * COLS + part * 32, 32), 32)
            for j in range(4):
                found = [col_term[slot_of[i * 4 + j], rows, :] for i in range(4)]
                col_send[t, j, part * 32 : part * 32 + 32] = (
                    (found[0] + found[1]) + (found[2] + found[3])
                ).astype(BF16)

    def add(p, m):
        for side in range(2):
            row_sum[m, side] = (
                row_send[core, m, side].astype(F32) + row_half[p, m, side].astype(F32)
            ).astype(BF16)

    def col_add(p, t, crossed):
        for j in range(4):
            total = col_send[t, j].astype(F32)
            for q in crossed:
                total = total + col_cross[p, q, j].astype(F32)
            col_send[t, j] = total.astype(BF16)

    def scatter(p):
        loop(NEAR, 8, row_part)
        sibling_send(p, 1).start()
        col_part((1 - xl) * NY + lax.rem(y + 2, NY))
        cross_send(p, 2).start()
        loop(0, NEAR, row_part)
        sibling_send(p, 0).start()
        for q in (1, 3):
            col_part((1 - xl) * NY + lax.rem(y + q, NY))
            cross_send(p, q).start()
        sibling_send(p, 1).wait_recv()
        for m in range(NEAR, 8):
            add(p, m)
        for send in far_sends(p):
            send.start()
        col_part(xl * NY + lax.rem(y + 2, NY))
        col_part(across)
        sibling_send(p, 0).wait_recv()
        for m in range(NEAR):
            add(p, m)
        for send in near_sends(p, (1, 2, 0)):
            send.start()
        for q in (1, 3):
            col_part(xl * NY + lax.rem(y + q, NY))
            straight_send(p, q).start()
        col_part(r)
        cross_send(p, 2).wait_recv()
        col_add(p, xl * NY + lax.rem(y + 2, NY), (2,))
        straight_send(p, 2).start()
        for q in (1, 3):
            cross_send(p, q).wait_recv()
        col_add(p, across, (1, 3))
        across_send(p).start()
        for send in far_sends(p):
            send.wait_recv()
        for m, e in ((3, 0), (4, 1)):
            for side in range(2):
                total = row_sum[m, side].astype(F32) + row_far[p, e, side].astype(F32)
                if side == e:
                    total = total + row_last[p, e].astype(F32)
                row_sum[m, side] = total.astype(BF16)
        for send in near_sends(p, (3, 4)):
            send.start()

    def row_update(p):
        for send in near_sends(p, range(NEAR)):
            send.wait_recv()
        total = row_sum[0, xh].astype(F32)
        for sem in range(1, 2 * NEAR):
            total = total + row_got[p, sem].astype(F32)
        row_now[...] = row_now[...] - 0.0004 * total

    def col_update(p):
        for q in ys:
            straight_send(p, q).wait_recv()
        across_send(p).wait_recv()
        for j in range(4):
            total = col_send[r, j].astype(F32)
            for q in range(NY):
                total = total + col_got[p, q, j].astype(F32)
            col_now[j] = col_now[j] - 0.0004 * total

    def scatter_sent(p):
        for q in ys:
            cross_send(p, q).wait_send()
            straight_send(p, q).wait_send()
        across_send(p).wait_send()
        for send in far_sends(p) + near_sends(p, range(NEAR)):
            send.wait_send()
        for part in range(2):
            sibling_send(p, part).wait_send()

    tiles(0)
    scatter(0)
    row_update(0)
    row_round(1)
    row_gather_send(1)
    col_update(0)
    col_round(1)
    col_gather_send(1)
    scatter_sent(0)
    pass_on(1)
    pass_back(1)
    relay(1)
    hand_near(1)
    hand_far(1)
    gather_end(1)
    arrange(1)
    tiles(1)
    scatter(1)
    row_update(1)
    row_back = pltpu.make_async_copy(row_now, row_out, out_sem.at[0])
    row_back.start()
    col_update(1)
    col_back = pltpu.make_async_copy(col_now, col_out, out_sem.at[1])
    col_back.start()
    scatter_sent(1)
    gather_sent(0)
    gather_sent(1)
    row_back.wait()
    col_back.wait()


def finish(row_ref, col_ref, row_out, col_out, row_now, col_now, sem):
    ways = [(row_ref, row_now, row_out), (col_ref, col_now, col_out)]
    coming = [pltpu.make_async_copy(src, now, sem.at[k]) for k, (src, now, _) in enumerate(ways)]
    going = [pltpu.make_async_copy(now, dst, sem.at[2 + k]) for k, (_, now, dst) in enumerate(ways)]
    for copy in coming:
        copy.start()
    for k in range(2):
        coming[k].wait()
        going[k].start()
    for copy in going:
        copy.wait()


def shards(row_emb, col_emb, row_marg, col_marg, tile_list, tile_count, tile_data):
    vmem = pl.BlockSpec(memory_space=pltpu.VMEM)
    smem = pl.BlockSpec(memory_space=pltpu.SMEM)
    dma = pltpu.SemaphoreType.DMA
    where = pl.BlockSpec(memory_space=pl.ANY)
    news = pl.pallas_call(
        kernel,
        out_shape=(
            jax.ShapeDtypeStruct(row_emb.shape, F32),
            jax.ShapeDtypeStruct(col_emb.shape, F32),
        ),
        in_specs=[smem, smem, where, where, vmem, vmem, where],
        out_specs=(where, where),
        scratch_shapes=[
            pltpu.VMEM(row_emb.shape, F32),
            pltpu.VMEM(col_emb.shape, F32),
            pltpu.VMEM((2, 2, 8, 2, 5, ROWS, K), BF16),
            pltpu.VMEM((2, NROW, 17, 16, K), BF16),
            pltpu.VMEM((4, B, K), BF16),
            pltpu.VMEM((2, 16, K), F32),
            pltpu.VMEM((4, B, 128), BF16),
            pltpu.VMEM((4, B, 128), F32),
            pltpu.VMEM((16, B), F32),
            pltpu.VMEM((SLOTS, B, B), BF16),
            pltpu.VMEM((SLOTS, B, B), BF16),
            pltpu.VMEM((SLOTS, B, B), jnp.int32),
            pltpu.VMEM((SLOTS + 1, B, K), F32),
            pltpu.VMEM((SLOTS + 1, B, K), F32),
            pltpu.VMEM((2, 8, 2, 4, ROWS, K), BF16),
            pltpu.VMEM((2, 8, 2, 4, ROWS, K), BF16),
            pltpu.VMEM((8, 2, 4, ROWS, K), BF16),
            pltpu.VMEM((2, 2, 2, 4, ROWS, K), BF16),
            pltpu.VMEM((2, 2, 4, ROWS, K), BF16),
            pltpu.VMEM((2, 2 * NEAR, 4, ROWS, K), BF16),
            pltpu.VMEM((NROW, 4, COLS, K), BF16),
            pltpu.VMEM((2, NY, 4, COLS, K), BF16),
            pltpu.VMEM((2, NY, 4, COLS, K), BF16),
            pltpu.SMEM((16,), jnp.int32),
            pltpu.SMEM((SLOTS, 2), jnp.int32),
            dma((SLOTS,)), dma((2,)), dma((2,)),
            dma((2, 14)), dma((2, 14)), dma((2, 2)), dma((2, 2)), dma((2, NROW)), dma((2, NROW)),
            dma((2, 2)), dma((2, 2)), dma((2, 14)), dma((2, 14)), dma((2, NROW)), dma((2, NROW)),
        ],
        name="swivel",
        compiler_params=pltpu.CompilerParams(
            collective_id=0, has_side_effects=True, vmem_limit_bytes=60 * 2**20
        ),
        cost_estimate=pl.CostEstimate(flops=6_400_000_000, bytes_accessed=9_000_000, transcendentals=8_000_000),
    )(tile_count, tile_list[0, 0].T, row_emb, col_emb, row_marg, col_marg, tile_data)
    return pl.pallas_call(
        finish,
        out_shape=tuple(jax.ShapeDtypeStruct(new.shape, F32) for new in news),
        in_specs=[where, where],
        out_specs=(where, where),
        scratch_shapes=[pltpu.VMEM(new.shape, F32) for new in news] + [dma((4,))],
        name="finish",
    )(*news)


def solution(mesh):
    placed = (
        P("row", "col", None),
        P("col", "row", None),
        P("row", "col"),
        P("col", "row"),
        P("row", "col", None, None),
        P("row", "col"),
        P("row", "col", None, None, None),
    )
    return jax.shard_map(
        shards,
        mesh=mesh,
        in_specs=placed,
        out_specs=(P("row", "col", None), P("col", "row", None)),
        check_vma=False,
    )
```

```python
import functools

import jax
import jax.numpy as jnp
from jax import lax
from jax.experimental import pallas as pl
from jax.experimental.pallas import tpu as pltpu
from jax.sharding import PartitionSpec as P

MESH = pl.DeviceIdType.MESH
BF16, F32 = jnp.bfloat16, jnp.float32
B, K = 512, 256
SLOTS = 8
NY = 4
NROW = 8
NZ = 8
NZX = 16
ROWS, COLS = 16, 64
NEAR = 5


def offset(n):
    odd = lax.rem(n, 2) if not isinstance(n, int) else n % 2
    return odd * ((n + 1) // 2) - (1 - odd) * (n // 2)


def kernel(
    count_ref, list_ref, row_ref, col_ref, rowm_ref, colm_ref, data_ref, row_out, col_out, row_now, col_now,
    row_got_panel, col_panel, row_panel, tile_f32, picked, marg_left, marg_right, bias, weight,
    stage, row_term, col_term, row_send, row_half, row_sum, row_far, row_last, row_got,
    col_send, col_cross, col_got, slot_of, pair_of,
    data_sem, in_sem, out_sem, rp_s, rp_r, rf_s, rf_r, cp_s, cp_r,
    sib_s, sib_r, rg_s, rg_r, cg_s, cg_r,
):
    r, c = lax.axis_index("row"), lax.axis_index("col")
    xl, y = r // NY, lax.rem(r, NY)
    zx, core = c // 2, lax.rem(c, 2)
    z, xh = zx // 2, lax.rem(zx, 2)
    sibling = {"row": r, "col": zx * 2 + (1 - core)}
    across = (1 - xl) * NY + y

    def at_z(dz, other=0):
        side = xh if other == 0 else 1 - xh
        return {"row": r, "col": (lax.rem(z + dz + NZ, NZ) * 2 + side) * 2 + core}

    def at_y(dy):
        return {"row": xl * NY + lax.rem(y + dy, NY), "col": c}

    def at_x():
        return {"row": across, "col": c}

    def copy(src, dst, send, recv, device):
        return pltpu.make_async_remote_copy(
            src_ref=src, dst_ref=dst, send_sem=send, recv_sem=recv, device_id=device, device_id_type=MESH
        )

    def loop(lo, hi, body):
        def step(i, carry):
            body(i)
            return carry

        lax.fori_loop(lo, hi, step, 0)

    barrier = pltpu.get_barrier_semaphore()
    partners = [at_z(dz, other) for dz in (2, -2, 1, -1) for other in (0, 1)] + [at_z(0, 1)]
    partners += [at_y(dy) for dy in (2, 1, 3)] + [at_x(), sibling]
    for device in partners:
        pl.semaphore_signal(barrier, inc=1, device_id=device, device_id_type=MESH)

    def data_copy(s):
        return pltpu.make_async_copy(data_ref.at[0, 0, s], stage.at[s], data_sem.at[s])

    row_in = pltpu.make_async_copy(row_ref, row_now, in_sem.at[0])
    col_in = pltpu.make_async_copy(col_ref, col_now, in_sem.at[1])
    row_in.start()
    col_in.start()
    loop(0, SLOTS, lambda s: data_copy(s).start())

    tile_f32[...] = jnp.zeros((2, 16, K), F32)
    tile_f32[0, 0:4, 0:ROWS] = rowm_ref[...].astype(F32)
    tile_f32[1, 0:4, 0:COLS] = colm_ref[...].astype(F32)
    row_got_panel[0, core, 0, xh, 4] = tile_f32[0].astype(BF16)
    col_panel[0, r, 16] = tile_f32[1].astype(BF16)
    row_in.wait()
    col_in.wait()

    def pieces(p):
        return pl.ds(0, 5 if p == 0 else 4)

    def col_rows(p):
        return pl.ds(0, 17 if p == 0 else 16)

    def row_direct(p):
        mine = row_got_panel.at[p, core, 0, xh, pieces(p)]
        out = []
        for n, other in ((3, 0), (4, 0), (3, 1), (4, 1), (1, 0), (2, 0), (0, 1), (1, 1), (2, 1)):
            sem = n * 2 + other
            there = row_got_panel.at[p, core, n, xh, pieces(p)]
            side = xh if other == 0 else 1 - xh
            here = row_got_panel.at[p, core, n, side, pieces(p)]
            device = at_z(offset(n), other)
            send = functools.partial(copy, mine, there, rp_s.at[p, sem], rp_r.at[p, sem], device)
            recv = functools.partial(copy, here, here, rp_s.at[p, sem], rp_r.at[p, sem], device)
            out.append(((n, other), send, recv))
        return out

    def row_relay(p, k):
        src, dst, dz, other = ((3, 5, 1, 0), (3, 7, 2, 0), (4, 6, -1, 0), (3, 5, 1, 1), (4, 6, -1, 1), (4, 7, -2, 1))[k]
        side = xh if other == 0 else 1 - xh
        here = row_got_panel.at[p, core, src, side, pieces(p)]
        there = row_got_panel.at[p, core, dst, side, pieces(p)]
        return copy(here, there, rp_s.at[p, 10 + k], rp_r.at[p, 10 + k], at_z(dz))

    def row_hand(p, part, side):
        slots = pl.ds(0, NEAR) if part == 0 else pl.ds(NEAR + part - 1, 1)
        block = row_got_panel.at[p, side, slots, :, pieces(p)]
        return copy(block, block, rf_s.at[p, part], rf_r.at[p, part], sibling)

    def col_direct(p, q):
        mine = col_panel.at[p, r, col_rows(p)]
        device = at_x() if q == NY else at_y(q)
        return copy(mine, mine, cp_s.at[p, q], cp_r.at[p, q], device)

    def col_direct_got(p, q):
        source = across if q == NY else xl * NY + lax.rem(y - q + NY, NY)
        got = col_panel.at[p, source, col_rows(p)]
        return copy(got, got, cp_s.at[p, q], cp_r.at[p, q], at_x())

    def col_pass(p, q):
        source = xl * NY + lax.rem(y + 2, NY) if q == 2 else across
        got = col_panel.at[p, source, col_rows(p)]
        return copy(got, got, cp_s.at[p, NY + q], cp_r.at[p, NY + q], at_x() if q == 2 else at_y(q))

    def col_pass_got(p, q):
        source = (1 - xl) * NY + lax.rem(y - q + NY, NY)
        got = col_panel.at[p, source, col_rows(p)]
        return copy(got, got, cp_s.at[p, NY + q], cp_r.at[p, NY + q], at_x())

    ys = (2, 1, 3)

    def col_gather_send(p):
        col_direct(p, NY).start()
        for q in ys:
            col_direct(p, q).start()

    def col_round(p):
        for j in range(4):
            col_panel[p, r, 4 * j : 4 * j + 4] = col_now[j].astype(BF16).reshape(4, 16, K)

    def row_round(p):
        row_got_panel[p, core, 0, xh, 0:4] = row_now[...].astype(BF16)

    def row_gather_send(p):
        for _, send, _ in row_direct(p):
            send().start()

    def pass_on(p):
        col_direct_got(p, NY).wait_recv()
        for q in (1, 3):
            col_pass(p, q).start()

    def pass_back(p):
        col_direct_got(p, 2).wait_recv()
        col_pass(p, 2).start()

    def row_direct_wait(p, *wanted):
        for which, _, recv in row_direct(p):
            if which in wanted:
                recv().wait_recv()

    def relay_own(p):
        row_direct_wait(p, (3, 0))
        row_relay(p, 0).start()
        row_relay(p, 1).start()
        row_direct_wait(p, (4, 0))
        row_relay(p, 2).start()

    def relay_other(p):
        row_direct_wait(p, (3, 1))
        row_relay(p, 3).start()
        row_direct_wait(p, (4, 1))
        row_relay(p, 4).start()
        row_relay(p, 5).start()

    def hand_near(p):
        row_direct_wait(p, (1, 0), (1, 1), (2, 0), (2, 1), (0, 1))
        row_hand(p, 0, core).start()

    def hand_far(p):
        for part, relays in ((1, (0, 3)), (2, (2, 4)), (3, (1, 5))):
            for k in relays:
                row_relay(p, k).wait_recv()
            row_hand(p, part, core).start()

    def gather_end(p):
        for q in (1, 3):
            col_direct_got(p, q).wait_recv()
        for q in ys:
            col_pass_got(p, q).wait_recv()
        for part in range(4):
            row_hand(p, part, 1 - core).wait_recv()

    def gather_sent(p):
        for _, send, _ in row_direct(p):
            send().wait_send()
        for k in range(6):
            row_relay(p, k).wait_send()
        for part in range(4):
            row_hand(p, part, core).wait_send()
        for q in (NY,) + ys:
            col_direct(p, q).wait_send()
        for q in ys:
            col_pass(p, q).wait_send()

    def arrange(p):
        def slot(n):
            source = lax.rem(z - offset(n) + 2 * NZ, NZ)
            for side in range(2):
                for k in range(2):
                    rows = pl.ds(pl.multiple_of(source * 64 + side * 32 + k * ROWS, ROWS), ROWS)
                    for i in range(4):
                        row_panel[i, rows, :] = row_got_panel[p, k, n, side, i]

        loop(0, 8, slot)

    col_round(0)
    row_round(0)
    pl.semaphore_wait(barrier, len(partners))
    col_gather_send(0)
    row_gather_send(0)

    row_term[SLOTS] = jnp.zeros((B, K), F32)
    col_term[SLOTS] = jnp.zeros((B, K), F32)
    codes = []
    for s in range(SLOTS):
        i = jnp.clip(list_ref[0, s] - r * 4, 0, 3)
        j = jnp.clip(list_ref[1, s] - c * 4, 0, 3)
        pair_of[s, 0] = i
        pair_of[s, 1] = j
        codes.append(jnp.where(s < count_ref[0, 0], i * 4 + j, -1))
    for pair in range(16):
        found = jnp.int32(SLOTS)
        for s in range(SLOTS):
            found = jnp.where(codes[s] == pair, s, found)
        slot_of[pair] = found

    def prepare(s):
        data_copy(s).wait()

        def part(h, carry):
            rows = pl.ds(pl.multiple_of(h * 64, 64), 64)
            level = stage[s, rows].astype(F32)
            bias[s, rows] = -jnp.log(jnp.maximum(level, 1.0)).astype(BF16)
            weight[s, rows] = jnp.where(level > 0.0, 0.1 + 0.25 * jnp.sqrt(level), 0.0).astype(BF16)
            return carry

        lax.fori_loop(0, B // 64, part, 0)

    loop(0, 3, prepare)
    relay_own(0)
    prepare(3)
    relay_other(0)
    pass_on(0)
    pass_back(0)
    prepare(4)
    hand_near(0)
    loop(5, SLOTS, prepare)
    hand_far(0)
    gather_end(0)
    arrange(0)

    lane = lax.broadcasted_iota(jnp.int32, (ROWS, 128), 1)
    mine = lane == lax.broadcasted_iota(jnp.int32, (ROWS, 128), 0)

    def pick(n):
        source = lax.rem(z - offset(n) + 2 * NZ, NZ)
        for side in range(2):
            for k in range(2):
                rows = pl.ds(pl.multiple_of(source * 64 + side * 32 + k * ROWS, ROWS), ROWS)
                margins = row_got_panel[0, k, n, side, 4].astype(F32)
                for i in range(4):
                    line = jnp.broadcast_to(margins[i : i + 1, 0:128], (ROWS, 128))
                    picked[i, rows, :] = jnp.where(mine, line, 0.0).astype(BF16)

    loop(0, 8, pick)
    ones = jnp.ones((128, 128), BF16)
    for i in range(4):
        marg_left[i] = jnp.dot(picked[i], ones, preferred_element_type=F32)
    for g in range(NROW // 2):
        low = col_panel[0, 2 * g, 16].astype(F32)[:, 0:128]
        high = col_panel[0, 2 * g + 1, 16].astype(F32)[:, 0:128]
        marg_right[:, g * 128 : (g + 1) * 128] = jnp.where(lane < COLS, low, pltpu.roll(high, COLS, 1))

    def tiles(p):
        def tile(s):
            i, j = pair_of[s, 0], pair_of[s, 1]
            col_piece = col_panel[p, :, pl.ds(4 * j, 4)].reshape(B, K)
            row_piece = row_panel[i]
            scores = lax.dot_general(row_piece, col_piece, (((1,), (1,)), ((), ())), preferred_element_type=F32)
            if p == 0:
                left = jnp.concatenate([marg_left[i]] * (B // 128), axis=1)
                shift = (bias[s].astype(F32) + marg_right[pl.ds(j, 1), :] + left).astype(BF16)
                bias[s] = shift
            else:
                shift = bias[s]
            diff = scores.astype(BF16) + shift
            scale = weight[s]
            signal = jnp.where(scale > 0, scale * diff, 0.5 * jnp.tanh(0.5 * diff) + 0.5).astype(BF16)
            row_term[s] = jnp.dot(signal, col_piece, preferred_element_type=F32)
            col_term[s] = lax.dot_general(signal, row_piece, (((0,), (0,)), ((), ())), preferred_element_type=F32)

        for s in range(SLOTS):
            tile(s)

    far, near = pl.ds(NEAR, 8 - NEAR), pl.ds(0, NEAR)

    def sibling_send(p, part):
        slots = near if part == 0 else far
        return copy(
            row_send.at[1 - core, slots], row_half.at[p, slots], sib_s.at[p, part], sib_r.at[p, part], sibling
        )

    def far_sends(p):
        return [
            copy(row_sum.at[7, 0], row_last.at[p, 0], rg_s.at[p, 12], rg_r.at[p, 12], at_z(2)),
            copy(row_sum.at[7, 1], row_last.at[p, 1], rg_s.at[p, 13], rg_r.at[p, 13], at_z(-2)),
            copy(row_sum.at[5], row_far.at[p, 0], rg_s.at[p, 10], rg_r.at[p, 10], at_z(1)),
            copy(row_sum.at[6], row_far.at[p, 1], rg_s.at[p, 11], rg_r.at[p, 11], at_z(-1)),
        ]

    def near_sends(p, slots):
        out = []
        for other in (1, 0):
            for m in slots:
                if m == 0 and other == 0:
                    continue
                sem = m * 2 + other
                side = xh if other == 0 else 1 - xh
                out.append(
                    copy(
                        row_sum.at[m, side], row_got.at[p, sem], rg_s.at[p, sem], rg_r.at[p, sem],
                        at_z(offset(m), other),
                    )
                )
        return out

    def cross_send(p, q):
        t = (1 - xl) * NY + lax.rem(y + q, NY)
        device = at_x() if q == 2 else at_y(q)
        return copy(col_send.at[t], col_cross.at[p, q], cg_s.at[p, NY + q], cg_r.at[p, NY + q], device)

    def straight_send(p, q):
        t = xl * NY + lax.rem(y + q, NY)
        return copy(col_send.at[t], col_got.at[p, q], cg_s.at[p, q], cg_r.at[p, q], at_y(q))

    def across_send(p):
        return copy(col_send.at[across], col_got.at[p, 0], cg_s.at[p, NY], cg_r.at[p, NY], at_x())

    def row_part(m):
        dest = lax.rem(z + offset(m) + NZ, NZ)
        for side in range(2):
            for k in range(2):
                rows = pl.ds(pl.multiple_of(dest * 64 + side * 32 + k * ROWS, ROWS), ROWS)
                for i in range(4):
                    found = [row_term[slot_of[i * 4 + j], rows, :] for j in range(4)]
                    row_send[k, m, side, i] = ((found[0] + found[1]) + (found[2] + found[3])).astype(BF16)

    def col_part(t):
        for part in range(2):
            rows = pl.ds(pl.multiple_of(t * COLS + part * 32, 32), 32)
            for j in range(4):
                found = [col_term[slot_of[i * 4 + j], rows, :] for i in range(4)]
                col_send[t, j, part * 32 : part * 32 + 32] = (
                    (found[0] + found[1]) + (found[2] + found[3])
                ).astype(BF16)

    def add(p, m):
        for side in range(2):
            row_sum[m, side] = (
                row_send[core, m, side].astype(F32) + row_half[p, m, side].astype(F32)
            ).astype(BF16)

    def col_add(p, t, crossed):
        for j in range(4):
            total = col_send[t, j].astype(F32)
            for q in crossed:
                total = total + col_cross[p, q, j].astype(F32)
            col_send[t, j] = total.astype(BF16)

    def scatter(p):
        loop(NEAR, 8, row_part)
        sibling_send(p, 1).start()
        col_part((1 - xl) * NY + lax.rem(y + 2, NY))
        cross_send(p, 2).start()
        loop(0, NEAR, row_part)
        sibling_send(p, 0).start()
        for q in (1, 3):
            col_part((1 - xl) * NY + lax.rem(y + q, NY))
            cross_send(p, q).start()
        sibling_send(p, 1).wait_recv()
        for m in range(NEAR, 8):
            add(p, m)
        for send in far_sends(p):
            send.start()
        col_part(xl * NY + lax.rem(y + 2, NY))
        col_part(across)
        sibling_send(p, 0).wait_recv()
        for m in range(NEAR):
            add(p, m)
        for send in near_sends(p, (1, 2, 0)):
            send.start()
        cross_send(p, 2).wait_recv()
        col_add(p, xl * NY + lax.rem(y + 2, NY), (2,))
        straight_send(p, 2).start()
        for q in (1, 3):
            col_part(xl * NY + lax.rem(y + q, NY))
        col_part(r)
        last_0, last_1, far_0, far_1 = far_sends(p)
        for m, e, sends in ((3, 0, (far_0, last_0)), (4, 1, (far_1, last_1))):
            for send in sends:
                send.wait_recv()
            for side in range(2):
                total = row_sum[m, side].astype(F32) + row_far[p, e, side].astype(F32)
                if side == e:
                    total = total + row_last[p, e].astype(F32)
                row_sum[m, side] = total.astype(BF16)
            for send in near_sends(p, (m,)):
                send.start()
        for q in (1, 3):
            cross_send(p, q).wait_recv()
        col_add(p, across, (1, 3))
        across_send(p).start()
        for q in (1, 3):
            straight_send(p, q).start()

    def row_update(p):
        for send in near_sends(p, range(NEAR)):
            send.wait_recv()
        total = row_sum[0, xh].astype(F32)
        for sem in range(1, 2 * NEAR):
            total = total + row_got[p, sem].astype(F32)
        row_now[...] = row_now[...] - 0.0004 * total

    def col_update(p):
        for q in ys:
            straight_send(p, q).wait_recv()
        across_send(p).wait_recv()
        for j in range(4):
            total = col_send[r, j].astype(F32)
            for q in range(NY):
                total = total + col_got[p, q, j].astype(F32)
            col_now[j] = col_now[j] - 0.0004 * total

    def scatter_sent(p):
        for q in ys:
            cross_send(p, q).wait_send()
            straight_send(p, q).wait_send()
        across_send(p).wait_send()
        for send in far_sends(p) + near_sends(p, range(NEAR)):
            send.wait_send()
        for part in range(2):
            sibling_send(p, part).wait_send()

    tiles(0)
    scatter(0)
    row_update(0)
    row_round(1)
    row_gather_send(1)
    col_update(0)
    col_round(1)
    col_gather_send(1)
    scatter_sent(0)
    relay_own(1)
    relay_other(1)
    pass_on(1)
    pass_back(1)
    hand_near(1)
    hand_far(1)
    gather_end(1)
    arrange(1)
    tiles(1)
    scatter(1)
    row_update(1)
    row_back = pltpu.make_async_copy(row_now, row_out, out_sem.at[0])
    row_back.start()
    col_update(1)
    col_back = pltpu.make_async_copy(col_now, col_out, out_sem.at[1])
    col_back.start()
    scatter_sent(1)
    gather_sent(0)
    gather_sent(1)
    row_back.wait()
    col_back.wait()


def finish(row_ref, col_ref, row_out, col_out, row_now, col_now, sem):
    ways = [(row_ref, row_now, row_out), (col_ref, col_now, col_out)]
    coming = [pltpu.make_async_copy(src, now, sem.at[k]) for k, (src, now, _) in enumerate(ways)]
    going = [pltpu.make_async_copy(now, dst, sem.at[2 + k]) for k, (_, now, dst) in enumerate(ways)]
    for copy in coming:
        copy.start()
    for k in range(2):
        coming[k].wait()
        going[k].start()
    for copy in going:
        copy.wait()


def shards(row_emb, col_emb, row_marg, col_marg, tile_list, tile_count, tile_data):
    vmem = pl.BlockSpec(memory_space=pltpu.VMEM)
    smem = pl.BlockSpec(memory_space=pltpu.SMEM)
    dma = pltpu.SemaphoreType.DMA
    where = pl.BlockSpec(memory_space=pl.ANY)
    news = pl.pallas_call(
        kernel,
        out_shape=(
            jax.ShapeDtypeStruct(row_emb.shape, F32),
            jax.ShapeDtypeStruct(col_emb.shape, F32),
        ),
        in_specs=[smem, smem, where, where, vmem, vmem, where],
        out_specs=(where, where),
        scratch_shapes=[
            pltpu.VMEM(row_emb.shape, F32),
            pltpu.VMEM(col_emb.shape, F32),
            pltpu.VMEM((2, 2, 8, 2, 5, ROWS, K), BF16),
            pltpu.VMEM((2, NROW, 17, 16, K), BF16),
            pltpu.VMEM((4, B, K), BF16),
            pltpu.VMEM((2, 16, K), F32),
            pltpu.VMEM((4, B, 128), BF16),
            pltpu.VMEM((4, B, 128), F32),
            pltpu.VMEM((16, B), F32),
            pltpu.VMEM((SLOTS, B, B), BF16),
            pltpu.VMEM((SLOTS, B, B), BF16),
            pltpu.VMEM((SLOTS, B, B), jnp.int32),
            pltpu.VMEM((SLOTS + 1, B, K), F32),
            pltpu.VMEM((SLOTS + 1, B, K), F32),
            pltpu.VMEM((2, 8, 2, 4, ROWS, K), BF16),
            pltpu.VMEM((2, 8, 2, 4, ROWS, K), BF16),
            pltpu.VMEM((8, 2, 4, ROWS, K), BF16),
            pltpu.VMEM((2, 2, 2, 4, ROWS, K), BF16),
            pltpu.VMEM((2, 2, 4, ROWS, K), BF16),
            pltpu.VMEM((2, 2 * NEAR, 4, ROWS, K), BF16),
            pltpu.VMEM((NROW, 4, COLS, K), BF16),
            pltpu.VMEM((2, NY, 4, COLS, K), BF16),
            pltpu.VMEM((2, NY, 4, COLS, K), BF16),
            pltpu.SMEM((16,), jnp.int32),
            pltpu.SMEM((SLOTS, 2), jnp.int32),
            dma((SLOTS,)), dma((2,)), dma((2,)),
            dma((2, 16)), dma((2, 16)), dma((2, 4)), dma((2, 4)), dma((2, NROW)), dma((2, NROW)),
            dma((2, 2)), dma((2, 2)), dma((2, 14)), dma((2, 14)), dma((2, NROW)), dma((2, NROW)),
        ],
        name="swivel",
        compiler_params=pltpu.CompilerParams(
            collective_id=0, has_side_effects=True, vmem_limit_bytes=60 * 2**20
        ),
        cost_estimate=pl.CostEstimate(flops=6_400_000_000, bytes_accessed=9_000_000, transcendentals=8_000_000),
    )(tile_count, tile_list[0, 0].T, row_emb, col_emb, row_marg, col_marg, tile_data)
    return pl.pallas_call(
        finish,
        out_shape=tuple(jax.ShapeDtypeStruct(new.shape, F32) for new in news),
        in_specs=[where, where],
        out_specs=(where, where),
        scratch_shapes=[pltpu.VMEM(new.shape, F32) for new in news] + [dma((4,))],
        name="finish",
    )(*news)


def solution(mesh):
    placed = (
        P("row", "col", None),
        P("col", "row", None),
        P("row", "col"),
        P("col", "row"),
        P("row", "col", None, None),
        P("row", "col"),
        P("row", "col", None, None, None),
    )
    return jax.shard_map(
        shards,
        mesh=mesh,
        in_specs=placed,
        out_specs=(P("row", "col", None), P("col", "row", None)),
        check_vma=False,
    )
```

```python
import functools

import jax
import jax.numpy as jnp
from jax import lax
from jax.experimental import pallas as pl
from jax.experimental.pallas import tpu as pltpu
from jax.sharding import PartitionSpec as P

MESH = pl.DeviceIdType.MESH
BF16, F32 = jnp.bfloat16, jnp.float32
B, K = 512, 256
SLOTS = 8
NY = 4
NROW = 8
NZ = 8
NZX = 16
ROWS, COLS = 16, 64
NEAR = 5


def offset(n):
    odd = lax.rem(n, 2) if not isinstance(n, int) else n % 2
    return odd * ((n + 1) // 2) - (1 - odd) * (n // 2)


def kernel(
    count_ref, list_ref, row_ref, col_ref, rowm_ref, colm_ref, data_ref, row_out, col_out, row_now, col_now,
    row_got_panel, col_panel, row_panel, tile_f32, picked, marg_left, marg_right, bias, weight,
    stage, signals, row_term, col_term, row_send, row_half, row_sum, row_far, row_last, row_got,
    col_send, col_cross, col_got, slot_of, pair_of,
    data_sem, in_sem, out_sem, rp_s, rp_r, rf_s, rf_r, cp_s, cp_r,
    sib_s, sib_r, rg_s, rg_r, cg_s, cg_r,
):
    r, c = lax.axis_index("row"), lax.axis_index("col")
    xl, y = r // NY, lax.rem(r, NY)
    zx, core = c // 2, lax.rem(c, 2)
    z, xh = zx // 2, lax.rem(zx, 2)
    sibling = {"row": r, "col": zx * 2 + (1 - core)}
    across = (1 - xl) * NY + y

    def at_z(dz, other=0):
        side = xh if other == 0 else 1 - xh
        return {"row": r, "col": (lax.rem(z + dz + NZ, NZ) * 2 + side) * 2 + core}

    def at_y(dy):
        return {"row": xl * NY + lax.rem(y + dy, NY), "col": c}

    def at_x():
        return {"row": across, "col": c}

    def copy(src, dst, send, recv, device):
        return pltpu.make_async_remote_copy(
            src_ref=src, dst_ref=dst, send_sem=send, recv_sem=recv, device_id=device, device_id_type=MESH
        )

    def loop(lo, hi, body):
        def step(i, carry):
            body(i)
            return carry

        lax.fori_loop(lo, hi, step, 0)

    barrier = pltpu.get_barrier_semaphore()
    partners = [at_z(dz, other) for dz in (2, -2, 1, -1) for other in (0, 1)] + [at_z(0, 1)]
    partners += [at_y(dy) for dy in (2, 1, 3)] + [at_x(), sibling]
    for device in partners:
        pl.semaphore_signal(barrier, inc=1, device_id=device, device_id_type=MESH)

    def data_copy(s):
        return pltpu.make_async_copy(data_ref.at[0, 0, s], stage.at[s], data_sem.at[s])

    row_in = pltpu.make_async_copy(row_ref, row_now, in_sem.at[0])
    col_in = pltpu.make_async_copy(col_ref, col_now, in_sem.at[1])
    row_in.start()
    col_in.start()
    loop(0, SLOTS, lambda s: data_copy(s).start())

    tile_f32[...] = jnp.zeros((2, 16, K), F32)
    tile_f32[0, 0:4, 0:ROWS] = rowm_ref[...].astype(F32)
    tile_f32[1, 0:4, 0:COLS] = colm_ref[...].astype(F32)
    row_got_panel[0, core, 0, xh, 4] = tile_f32[0].astype(BF16)
    col_panel[0, r, 16] = tile_f32[1].astype(BF16)
    row_in.wait()
    col_in.wait()

    def pieces(p):
        return pl.ds(0, 5 if p == 0 else 4)

    def col_rows(p):
        return pl.ds(0, 17 if p == 0 else 16)

    def row_direct(p):
        mine = row_got_panel.at[p, core, 0, xh, pieces(p)]
        out = []
        for n, other in ((3, 0), (4, 0), (3, 1), (4, 1), (1, 0), (2, 0), (0, 1), (1, 1), (2, 1)):
            sem = n * 2 + other
            there = row_got_panel.at[p, core, n, xh, pieces(p)]
            side = xh if other == 0 else 1 - xh
            here = row_got_panel.at[p, core, n, side, pieces(p)]
            device = at_z(offset(n), other)
            send = functools.partial(copy, mine, there, rp_s.at[p, sem], rp_r.at[p, sem], device)
            recv = functools.partial(copy, here, here, rp_s.at[p, sem], rp_r.at[p, sem], device)
            out.append(((n, other), send, recv))
        return out

    def row_relay(p, k):
        src, dst, dz, other = ((3, 5, 1, 0), (3, 7, 2, 0), (4, 6, -1, 0), (3, 5, 1, 1), (4, 6, -1, 1), (4, 7, -2, 1))[k]
        side = xh if other == 0 else 1 - xh
        here = row_got_panel.at[p, core, src, side, pieces(p)]
        there = row_got_panel.at[p, core, dst, side, pieces(p)]
        return copy(here, there, rp_s.at[p, 10 + k], rp_r.at[p, 10 + k], at_z(dz))

    def row_hand(p, part, side):
        slots = pl.ds(0, NEAR) if part == 0 else pl.ds(NEAR + part - 1, 1)
        block = row_got_panel.at[p, side, slots, :, pieces(p)]
        return copy(block, block, rf_s.at[p, part], rf_r.at[p, part], sibling)

    def col_direct(p, q):
        mine = col_panel.at[p, r, col_rows(p)]
        device = at_x() if q == NY else at_y(q)
        return copy(mine, mine, cp_s.at[p, q], cp_r.at[p, q], device)

    def col_direct_got(p, q):
        source = across if q == NY else xl * NY + lax.rem(y - q + NY, NY)
        got = col_panel.at[p, source, col_rows(p)]
        return copy(got, got, cp_s.at[p, q], cp_r.at[p, q], at_x())

    def col_pass(p, q):
        source = xl * NY + lax.rem(y + 2, NY) if q == 2 else across
        got = col_panel.at[p, source, col_rows(p)]
        return copy(got, got, cp_s.at[p, NY + q], cp_r.at[p, NY + q], at_x() if q == 2 else at_y(q))

    def col_pass_got(p, q):
        source = (1 - xl) * NY + lax.rem(y - q + NY, NY)
        got = col_panel.at[p, source, col_rows(p)]
        return copy(got, got, cp_s.at[p, NY + q], cp_r.at[p, NY + q], at_x())

    ys = (2, 1, 3)

    def col_gather_send(p):
        col_direct(p, NY).start()
        for q in ys:
            col_direct(p, q).start()

    def col_round(p):
        for j in range(4):
            col_panel[p, r, 4 * j : 4 * j + 4] = col_now[j].astype(BF16).reshape(4, 16, K)

    def row_round(p):
        row_got_panel[p, core, 0, xh, 0:4] = row_now[...].astype(BF16)

    def row_gather_send(p):
        for _, send, _ in row_direct(p):
            send().start()

    def pass_on(p):
        col_direct_got(p, NY).wait_recv()
        for q in (1, 3):
            col_pass(p, q).start()

    def pass_back(p):
        col_direct_got(p, 2).wait_recv()
        col_pass(p, 2).start()

    def row_direct_wait(p, *wanted):
        for which, _, recv in row_direct(p):
            if which in wanted:
                recv().wait_recv()

    def relay_own(p):
        row_direct_wait(p, (3, 0))
        row_relay(p, 0).start()
        row_relay(p, 1).start()
        row_direct_wait(p, (4, 0))
        row_relay(p, 2).start()

    def relay_other(p):
        row_direct_wait(p, (3, 1))
        row_relay(p, 3).start()
        row_direct_wait(p, (4, 1))
        row_relay(p, 4).start()
        row_relay(p, 5).start()

    def hand_near(p):
        row_direct_wait(p, (1, 0), (1, 1), (2, 0), (2, 1), (0, 1))
        row_hand(p, 0, core).start()

    def hand_far(p):
        for part, relays in ((1, (0, 3)), (2, (2, 4)), (3, (1, 5))):
            for k in relays:
                row_relay(p, k).wait_recv()
            row_hand(p, part, core).start()

    def gather_end(p):
        for q in (1, 3):
            col_direct_got(p, q).wait_recv()
        for q in ys:
            col_pass_got(p, q).wait_recv()
        row_hand(p, 0, 1 - core).wait_recv()

    def gather_far_end(p):
        for part in range(1, 4):
            row_hand(p, part, 1 - core).wait_recv()

    def gather_sent(p):
        for _, send, _ in row_direct(p):
            send().wait_send()
        for k in range(6):
            row_relay(p, k).wait_send()
        for part in range(4):
            row_hand(p, part, core).wait_send()
        for q in (NY,) + ys:
            col_direct(p, q).wait_send()
        for q in ys:
            col_pass(p, q).wait_send()

    def arrange(p, lo, hi):
        def slot(n):
            source = lax.rem(z - offset(n) + 2 * NZ, NZ)
            for side in range(2):
                for k in range(2):
                    rows = pl.ds(pl.multiple_of(source * 64 + side * 32 + k * ROWS, ROWS), ROWS)
                    for i in range(4):
                        row_panel[i, rows, :] = row_got_panel[p, k, n, side, i]

        loop(lo, hi, slot)

    col_round(0)
    row_round(0)
    pl.semaphore_wait(barrier, len(partners))
    col_gather_send(0)
    row_gather_send(0)

    row_term[SLOTS] = jnp.zeros((B, K), F32)
    col_term[SLOTS] = jnp.zeros((B, K), F32)
    codes = []
    for s in range(SLOTS):
        i = jnp.clip(list_ref[0, s] - r * 4, 0, 3)
        j = jnp.clip(list_ref[1, s] - c * 4, 0, 3)
        pair_of[s, 0] = i
        pair_of[s, 1] = j
        codes.append(jnp.where(s < count_ref[0, 0], i * 4 + j, -1))
    for pair in range(16):
        found = jnp.int32(SLOTS)
        for s in range(SLOTS):
            found = jnp.where(codes[s] == pair, s, found)
        slot_of[pair] = found

    def prepare(s):
        data_copy(s).wait()

        def part(h, carry):
            rows = pl.ds(pl.multiple_of(h * 64, 64), 64)
            level = stage[s, rows].astype(F32)
            bias[s, rows] = -jnp.log(jnp.maximum(level, 1.0)).astype(BF16)
            weight[s, rows] = jnp.where(level > 0.0, 0.1 + 0.25 * jnp.sqrt(level), 0.0).astype(BF16)
            return carry

        lax.fori_loop(0, B // 64, part, 0)

    loop(0, 3, prepare)
    relay_own(0)
    prepare(3)
    relay_other(0)
    pass_on(0)
    pass_back(0)
    prepare(4)
    hand_near(0)
    loop(5, SLOTS, prepare)
    hand_far(0)
    gather_end(0)
    arrange(0, 0, NEAR)

    lane = lax.broadcasted_iota(jnp.int32, (ROWS, 128), 1)
    mine = lane == lax.broadcasted_iota(jnp.int32, (ROWS, 128), 0)

    def pick(n):
        source = lax.rem(z - offset(n) + 2 * NZ, NZ)
        for side in range(2):
            for k in range(2):
                rows = pl.ds(pl.multiple_of(source * 64 + side * 32 + k * ROWS, ROWS), ROWS)
                margins = row_got_panel[0, k, n, side, 4].astype(F32)
                for i in range(4):
                    line = jnp.broadcast_to(margins[i : i + 1, 0:128], (ROWS, 128))
                    picked[i, rows, :] = jnp.where(mine, line, 0.0).astype(BF16)

    loop(0, NEAR, pick)
    for g in range(NROW // 2):
        low = col_panel[0, 2 * g, 16].astype(F32)[:, 0:128]
        high = col_panel[0, 2 * g + 1, 16].astype(F32)[:, 0:128]
        marg_right[:, g * 128 : (g + 1) * 128] = jnp.where(lane < COLS, low, pltpu.roll(high, COLS, 1))
    gather_far_end(0)
    arrange(0, NEAR, 8)
    loop(NEAR, 8, pick)
    ones = jnp.ones((128, 128), BF16)
    for i in range(4):
        marg_left[i] = jnp.dot(picked[i], ones, preferred_element_type=F32)

    def tiles(p):
        def tile(s):
            i, j = pair_of[s, 0], pair_of[s, 1]
            col_piece = col_panel[p, :, pl.ds(4 * j, 4)].reshape(B, K)
            row_piece = row_panel[i]
            scores = lax.dot_general(row_piece, col_piece, (((1,), (1,)), ((), ())), preferred_element_type=F32)
            if p == 0:
                left = jnp.concatenate([marg_left[i]] * (B // 128), axis=1)
                shift = (bias[s].astype(F32) + marg_right[pl.ds(j, 1), :] + left).astype(BF16)
                bias[s] = shift
            else:
                shift = bias[s]
            diff = scores.astype(BF16) + shift
            scale = weight[s]
            signal = jnp.where(scale > 0, scale * diff, 0.5 * jnp.tanh(0.5 * diff) + 0.5).astype(BF16)
            signals[s] = signal
            row_term[s] = jnp.dot(signal, col_piece, preferred_element_type=F32)

        for s in range(SLOTS):
            tile(s)

    def col_terms(lo, hi):
        for s in range(lo, hi):
            col_term[s] = lax.dot_general(
                signals[s], row_panel[pair_of[s, 0]], (((0,), (0,)), ((), ())), preferred_element_type=F32
            )

    far, near = pl.ds(NEAR, 8 - NEAR), pl.ds(0, NEAR)

    def sibling_send(p, part):
        slots = near if part == 0 else far
        return copy(
            row_send.at[1 - core, slots], row_half.at[p, slots], sib_s.at[p, part], sib_r.at[p, part], sibling
        )

    def far_sends(p):
        return [
            copy(row_sum.at[7, 0], row_last.at[p, 0], rg_s.at[p, 12], rg_r.at[p, 12], at_z(2)),
            copy(row_sum.at[7, 1], row_last.at[p, 1], rg_s.at[p, 13], rg_r.at[p, 13], at_z(-2)),
            copy(row_sum.at[5], row_far.at[p, 0], rg_s.at[p, 10], rg_r.at[p, 10], at_z(1)),
            copy(row_sum.at[6], row_far.at[p, 1], rg_s.at[p, 11], rg_r.at[p, 11], at_z(-1)),
        ]

    def near_sends(p, slots):
        out = []
        for other in (1, 0):
            for m in slots:
                if m == 0 and other == 0:
                    continue
                sem = m * 2 + other
                side = xh if other == 0 else 1 - xh
                out.append(
                    copy(
                        row_sum.at[m, side], row_got.at[p, sem], rg_s.at[p, sem], rg_r.at[p, sem],
                        at_z(offset(m), other),
                    )
                )
        return out

    def cross_send(p, q):
        t = (1 - xl) * NY + lax.rem(y + q, NY)
        device = at_x() if q == 2 else at_y(q)
        return copy(col_send.at[t], col_cross.at[p, q], cg_s.at[p, NY + q], cg_r.at[p, NY + q], device)

    def straight_send(p, q):
        t = xl * NY + lax.rem(y + q, NY)
        return copy(col_send.at[t], col_got.at[p, q], cg_s.at[p, q], cg_r.at[p, q], at_y(q))

    def across_send(p):
        return copy(col_send.at[across], col_got.at[p, 0], cg_s.at[p, NY], cg_r.at[p, NY], at_x())

    def row_part(m):
        dest = lax.rem(z + offset(m) + NZ, NZ)
        for side in range(2):
            for k in range(2):
                rows = pl.ds(pl.multiple_of(dest * 64 + side * 32 + k * ROWS, ROWS), ROWS)
                for i in range(4):
                    found = [row_term[slot_of[i * 4 + j], rows, :] for j in range(4)]
                    row_send[k, m, side, i] = ((found[0] + found[1]) + (found[2] + found[3])).astype(BF16)

    def col_part(t):
        for part in range(2):
            rows = pl.ds(pl.multiple_of(t * COLS + part * 32, 32), 32)
            for j in range(4):
                found = [col_term[slot_of[i * 4 + j], rows, :] for i in range(4)]
                col_send[t, j, part * 32 : part * 32 + 32] = (
                    (found[0] + found[1]) + (found[2] + found[3])
                ).astype(BF16)

    def add(p, m):
        for side in range(2):
            row_sum[m, side] = (
                row_send[core, m, side].astype(F32) + row_half[p, m, side].astype(F32)
            ).astype(BF16)

    def col_add(p, t, crossed):
        for j in range(4):
            total = col_send[t, j].astype(F32)
            for q in crossed:
                total = total + col_cross[p, q, j].astype(F32)
            col_send[t, j] = total.astype(BF16)

    def scatter(p):
        loop(NEAR, 8, row_part)
        sibling_send(p, 1).start()
        loop(0, NEAR, row_part)
        sibling_send(p, 0).start()
        col_terms(0, 4)
        sibling_send(p, 1).wait_recv()
        for m in range(NEAR, 8):
            add(p, m)
        for send in far_sends(p):
            send.start()
        col_terms(4, SLOTS)
        col_part((1 - xl) * NY + lax.rem(y + 2, NY))
        cross_send(p, 2).start()
        for q in (1, 3):
            col_part((1 - xl) * NY + lax.rem(y + q, NY))
            cross_send(p, q).start()
        sibling_send(p, 0).wait_recv()
        for m in range(NEAR):
            add(p, m)
        for send in near_sends(p, (1, 2, 0)):
            send.start()
        col_part(xl * NY + lax.rem(y + 2, NY))
        col_part(across)
        cross_send(p, 2).wait_recv()
        col_add(p, xl * NY + lax.rem(y + 2, NY), (2,))
        straight_send(p, 2).start()
        for q in (1, 3):
            col_part(xl * NY + lax.rem(y + q, NY))
        col_part(r)
        last_0, last_1, far_0, far_1 = far_sends(p)
        for m, e, sends in ((3, 0, (far_0, last_0)), (4, 1, (far_1, last_1))):
            for send in sends:
                send.wait_recv()
            for side in range(2):
                total = row_sum[m, side].astype(F32) + row_far[p, e, side].astype(F32)
                if side == e:
                    total = total + row_last[p, e].astype(F32)
                row_sum[m, side] = total.astype(BF16)
            for send in near_sends(p, (m,)):
                send.start()
        for q in (1, 3):
            cross_send(p, q).wait_recv()
        col_add(p, across, (1, 3))
        across_send(p).start()
        for q in (1, 3):
            straight_send(p, q).start()

    def row_update(p):
        for send in near_sends(p, range(NEAR)):
            send.wait_recv()
        total = row_sum[0, xh].astype(F32)
        for sem in range(1, 2 * NEAR):
            total = total + row_got[p, sem].astype(F32)
        row_now[...] = row_now[...] - 0.0004 * total

    def col_update(p):
        for q in ys:
            straight_send(p, q).wait_recv()
        across_send(p).wait_recv()
        for j in range(4):
            total = col_send[r, j].astype(F32)
            for q in range(NY):
                total = total + col_got[p, q, j].astype(F32)
            col_now[j] = col_now[j] - 0.0004 * total

    def scatter_sent(p):
        for q in ys:
            cross_send(p, q).wait_send()
            straight_send(p, q).wait_send()
        across_send(p).wait_send()
        for send in far_sends(p) + near_sends(p, range(NEAR)):
            send.wait_send()
        for part in range(2):
            sibling_send(p, part).wait_send()

    tiles(0)
    scatter(0)
    row_update(0)
    row_round(1)
    row_gather_send(1)
    col_update(0)
    col_round(1)
    col_gather_send(1)
    scatter_sent(0)
    relay_own(1)
    relay_other(1)
    pass_on(1)
    pass_back(1)
    hand_near(1)
    hand_far(1)
    gather_end(1)
    arrange(1, 0, NEAR)
    gather_far_end(1)
    arrange(1, NEAR, 8)
    tiles(1)
    scatter(1)
    row_update(1)
    row_back = pltpu.make_async_copy(row_now, row_out, out_sem.at[0])
    row_back.start()
    col_update(1)
    col_back = pltpu.make_async_copy(col_now, col_out, out_sem.at[1])
    col_back.start()
    scatter_sent(1)
    gather_sent(0)
    gather_sent(1)
    row_back.wait()
    col_back.wait()


def finish(row_ref, col_ref, row_out, col_out, row_now, col_now, sem):
    ways = [(row_ref, row_now, row_out), (col_ref, col_now, col_out)]
    coming = [pltpu.make_async_copy(src, now, sem.at[k]) for k, (src, now, _) in enumerate(ways)]
    going = [pltpu.make_async_copy(now, dst, sem.at[2 + k]) for k, (_, now, dst) in enumerate(ways)]
    for copy in coming:
        copy.start()
    for k in range(2):
        coming[k].wait()
        going[k].start()
    for copy in going:
        copy.wait()


def shards(row_emb, col_emb, row_marg, col_marg, tile_list, tile_count, tile_data):
    vmem = pl.BlockSpec(memory_space=pltpu.VMEM)
    smem = pl.BlockSpec(memory_space=pltpu.SMEM)
    dma = pltpu.SemaphoreType.DMA
    where = pl.BlockSpec(memory_space=pl.ANY)
    news = pl.pallas_call(
        kernel,
        out_shape=(
            jax.ShapeDtypeStruct(row_emb.shape, F32),
            jax.ShapeDtypeStruct(col_emb.shape, F32),
        ),
        in_specs=[smem, smem, where, where, vmem, vmem, where],
        out_specs=(where, where),
        scratch_shapes=[
            pltpu.VMEM(row_emb.shape, F32),
            pltpu.VMEM(col_emb.shape, F32),
            pltpu.VMEM((2, 2, 8, 2, 5, ROWS, K), BF16),
            pltpu.VMEM((2, NROW, 17, 16, K), BF16),
            pltpu.VMEM((4, B, K), BF16),
            pltpu.VMEM((2, 16, K), F32),
            pltpu.VMEM((4, B, 128), BF16),
            pltpu.VMEM((4, B, 128), F32),
            pltpu.VMEM((16, B), F32),
            pltpu.VMEM((SLOTS, B, B), BF16),
            pltpu.VMEM((SLOTS, B, B), BF16),
            pltpu.VMEM((SLOTS, B, B), jnp.int32),
            pltpu.VMEM((SLOTS, B, B), BF16),
            pltpu.VMEM((SLOTS + 1, B, K), F32),
            pltpu.VMEM((SLOTS + 1, B, K), F32),
            pltpu.VMEM((2, 8, 2, 4, ROWS, K), BF16),
            pltpu.VMEM((2, 8, 2, 4, ROWS, K), BF16),
            pltpu.VMEM((8, 2, 4, ROWS, K), BF16),
            pltpu.VMEM((2, 2, 2, 4, ROWS, K), BF16),
            pltpu.VMEM((2, 2, 4, ROWS, K), BF16),
            pltpu.VMEM((2, 2 * NEAR, 4, ROWS, K), BF16),
            pltpu.VMEM((NROW, 4, COLS, K), BF16),
            pltpu.VMEM((2, NY, 4, COLS, K), BF16),
            pltpu.VMEM((2, NY, 4, COLS, K), BF16),
            pltpu.SMEM((16,), jnp.int32),
            pltpu.SMEM((SLOTS, 2), jnp.int32),
            dma((SLOTS,)), dma((2,)), dma((2,)),
            dma((2, 16)), dma((2, 16)), dma((2, 4)), dma((2, 4)), dma((2, NROW)), dma((2, NROW)),
            dma((2, 2)), dma((2, 2)), dma((2, 14)), dma((2, 14)), dma((2, NROW)), dma((2, NROW)),
        ],
        name="swivel",
        compiler_params=pltpu.CompilerParams(
            collective_id=0, has_side_effects=True, vmem_limit_bytes=60 * 2**20
        ),
        cost_estimate=pl.CostEstimate(flops=6_400_000_000, bytes_accessed=9_000_000, transcendentals=8_000_000),
    )(tile_count, tile_list[0, 0].T, row_emb, col_emb, row_marg, col_marg, tile_data)
    return pl.pallas_call(
        finish,
        out_shape=tuple(jax.ShapeDtypeStruct(new.shape, F32) for new in news),
        in_specs=[where, where],
        out_specs=(where, where),
        scratch_shapes=[pltpu.VMEM(new.shape, F32) for new in news] + [dma((4,))],
        name="finish",
    )(*news)


def solution(mesh):
    placed = (
        P("row", "col", None),
        P("col", "row", None),
        P("row", "col"),
        P("col", "row"),
        P("row", "col", None, None),
        P("row", "col"),
        P("row", "col", None, None, None),
    )
    return jax.shard_map(
        shards,
        mesh=mesh,
        in_specs=placed,
        out_specs=(P("row", "col", None), P("col", "row", None)),
        check_vma=False,
    )
```

```python
import functools

import jax
import jax.numpy as jnp
from jax import lax
from jax.experimental import pallas as pl
from jax.experimental.pallas import tpu as pltpu
from jax.sharding import PartitionSpec as P

MESH = pl.DeviceIdType.MESH
BF16, F32 = jnp.bfloat16, jnp.float32
B, K = 512, 256
SLOTS = 8
NY = 4
NROW = 8
NZ = 8
NZX = 16
ROWS, COLS = 16, 64
NEAR = 5


def offset(n):
    odd = lax.rem(n, 2) if not isinstance(n, int) else n % 2
    return odd * ((n + 1) // 2) - (1 - odd) * (n // 2)


def kernel(
    count_ref, list_ref, row_ref, col_ref, rowm_ref, colm_ref, data_ref, row_out, col_out, row_now, col_now,
    row_got_panel, col_panel, row_panel, tile_f32, picked, marg_left, marg_right, bias, weight,
    stage, signals, row_term, col_term, row_send, row_half, row_sum, row_far, row_last, row_got,
    col_send, col_cross, col_got, slot_of, pair_of,
    data_sem, in_sem, out_sem, rp_s, rp_r, rf_s, rf_r, cp_s, cp_r,
    sib_s, sib_r, rg_s, rg_r, cg_s, cg_r,
):
    r, c = lax.axis_index("row"), lax.axis_index("col")
    xl, y = r // NY, lax.rem(r, NY)
    zx, core = c // 2, lax.rem(c, 2)
    z, xh = zx // 2, lax.rem(zx, 2)
    sibling = {"row": r, "col": zx * 2 + (1 - core)}
    across = (1 - xl) * NY + y

    def at_z(dz, other=0):
        side = xh if other == 0 else 1 - xh
        return {"row": r, "col": (lax.rem(z + dz + NZ, NZ) * 2 + side) * 2 + core}

    def at_y(dy):
        return {"row": xl * NY + lax.rem(y + dy, NY), "col": c}

    def at_x():
        return {"row": across, "col": c}

    def copy(src, dst, send, recv, device):
        return pltpu.make_async_remote_copy(
            src_ref=src, dst_ref=dst, send_sem=send, recv_sem=recv, device_id=device, device_id_type=MESH
        )

    def loop(lo, hi, body):
        def step(i, carry):
            body(i)
            return carry

        lax.fori_loop(lo, hi, step, 0)

    barrier = pltpu.get_barrier_semaphore()
    partners = [at_z(dz, other) for dz in (2, -2, 1, -1) for other in (0, 1)] + [at_z(0, 1)]
    partners += [at_y(dy) for dy in (2, 1, 3)] + [at_x(), sibling]
    for device in partners:
        pl.semaphore_signal(barrier, inc=1, device_id=device, device_id_type=MESH)

    def data_copy(s):
        return pltpu.make_async_copy(data_ref.at[0, 0, s], stage.at[s], data_sem.at[s])

    row_in = pltpu.make_async_copy(row_ref, row_now, in_sem.at[0])
    col_in = pltpu.make_async_copy(col_ref, col_now, in_sem.at[1])
    row_in.start()
    col_in.start()
    loop(0, SLOTS, lambda s: data_copy(s).start())

    tile_f32[...] = jnp.zeros((2, 16, K), F32)
    tile_f32[0, 0:4, 0:ROWS] = rowm_ref[...].astype(F32)
    tile_f32[1, 0:4, 0:COLS] = colm_ref[...].astype(F32)
    row_got_panel[0, core, 0, xh, 4] = tile_f32[0].astype(BF16)
    col_panel[0, r, 16] = tile_f32[1].astype(BF16)
    row_in.wait()
    col_in.wait()

    def pieces(p):
        return pl.ds(0, 5 if p == 0 else 4)

    def col_rows(p):
        return pl.ds(0, 17 if p == 0 else 16)

    def row_direct(p):
        mine = row_got_panel.at[p, core, 0, xh, pieces(p)]
        out = []
        for n, other in ((3, 0), (4, 0), (3, 1), (4, 1), (1, 0), (2, 0), (0, 1), (1, 1), (2, 1)):
            sem = n * 2 + other
            there = row_got_panel.at[p, core, n, xh, pieces(p)]
            side = xh if other == 0 else 1 - xh
            here = row_got_panel.at[p, core, n, side, pieces(p)]
            device = at_z(offset(n), other)
            send = functools.partial(copy, mine, there, rp_s.at[p, sem], rp_r.at[p, sem], device)
            recv = functools.partial(copy, here, here, rp_s.at[p, sem], rp_r.at[p, sem], device)
            out.append(((n, other), send, recv))
        return out

    def row_relay(p, k):
        src, dst, dz, other = ((3, 5, 1, 0), (3, 7, 2, 0), (4, 6, -1, 0), (3, 5, 1, 1), (4, 6, -1, 1), (4, 7, -2, 1))[k]
        side = xh if other == 0 else 1 - xh
        here = row_got_panel.at[p, core, src, side, pieces(p)]
        there = row_got_panel.at[p, core, dst, side, pieces(p)]
        return copy(here, there, rp_s.at[p, 10 + k], rp_r.at[p, 10 + k], at_z(dz))

    def row_hand(p, part, side):
        slots = pl.ds(0, NEAR) if part == 0 else pl.ds(NEAR + part - 1, 1)
        block = row_got_panel.at[p, side, slots, :, pieces(p)]
        return copy(block, block, rf_s.at[p, part], rf_r.at[p, part], sibling)

    def col_direct(p, q):
        mine = col_panel.at[p, r, col_rows(p)]
        device = at_x() if q == NY else at_y(q)
        return copy(mine, mine, cp_s.at[p, q], cp_r.at[p, q], device)

    def col_direct_got(p, q):
        source = across if q == NY else xl * NY + lax.rem(y - q + NY, NY)
        got = col_panel.at[p, source, col_rows(p)]
        return copy(got, got, cp_s.at[p, q], cp_r.at[p, q], at_x())

    def col_pass(p, q):
        source = xl * NY + lax.rem(y + 2, NY) if q == 2 else across
        got = col_panel.at[p, source, col_rows(p)]
        return copy(got, got, cp_s.at[p, NY + q], cp_r.at[p, NY + q], at_x() if q == 2 else at_y(q))

    def col_pass_got(p, q):
        source = (1 - xl) * NY + lax.rem(y - q + NY, NY)
        got = col_panel.at[p, source, col_rows(p)]
        return copy(got, got, cp_s.at[p, NY + q], cp_r.at[p, NY + q], at_x())

    ys = (2, 1, 3)

    def col_gather_send(p):
        col_direct(p, NY).start()
        for q in ys:
            col_direct(p, q).start()

    def col_round(p):
        for j in range(4):
            col_panel[p, r, 4 * j : 4 * j + 4] = col_now[j].astype(BF16).reshape(4, 16, K)

    def row_round(p):
        row_got_panel[p, core, 0, xh, 0:4] = row_now[...].astype(BF16)

    def row_gather_send(p):
        for _, send, _ in row_direct(p):
            send().start()

    def pass_on(p):
        col_direct_got(p, NY).wait_recv()
        for q in (1, 3):
            col_pass(p, q).start()

    def pass_back(p):
        col_direct_got(p, 2).wait_recv()
        col_pass(p, 2).start()

    def row_direct_wait(p, *wanted):
        for which, _, recv in row_direct(p):
            if which in wanted:
                recv().wait_recv()

    def relay_own(p):
        row_direct_wait(p, (3, 0))
        row_relay(p, 0).start()
        row_relay(p, 1).start()
        row_direct_wait(p, (4, 0))
        row_relay(p, 2).start()

    def relay_other(p):
        row_direct_wait(p, (3, 1))
        row_relay(p, 3).start()
        row_direct_wait(p, (4, 1))
        row_relay(p, 4).start()
        row_relay(p, 5).start()

    def hand_near(p):
        row_direct_wait(p, (1, 0), (1, 1), (2, 0), (2, 1), (0, 1))
        row_hand(p, 0, core).start()

    def hand_far(p):
        for part, relays in ((1, (0, 3)), (2, (2, 4)), (3, (1, 5))):
            for k in relays:
                row_relay(p, k).wait_recv()
            row_hand(p, part, core).start()

    def gather_end(p):
        for q in (1, 3):
            col_direct_got(p, q).wait_recv()
        for q in ys:
            col_pass_got(p, q).wait_recv()
        for part in range(4):
            row_hand(p, part, 1 - core).wait_recv()

    def gather_sent(p):
        for _, send, _ in row_direct(p):
            send().wait_send()
        for k in range(6):
            row_relay(p, k).wait_send()
        for part in range(4):
            row_hand(p, part, core).wait_send()
        for q in (NY,) + ys:
            col_direct(p, q).wait_send()
        for q in ys:
            col_pass(p, q).wait_send()

    def arrange(p):
        def slot(n):
            source = lax.rem(z - offset(n) + 2 * NZ, NZ)
            for side in range(2):
                for k in range(2):
                    rows = pl.ds(pl.multiple_of(source * 64 + side * 32 + k * ROWS, ROWS), ROWS)
                    for i in range(4):
                        row_panel[i, rows, :] = row_got_panel[p, k, n, side, i]

        loop(0, 8, slot)

    col_round(0)
    row_round(0)
    pl.semaphore_wait(barrier, len(partners))
    col_gather_send(0)
    row_gather_send(0)

    row_term[SLOTS] = jnp.zeros((B, K), F32)
    col_term[SLOTS] = jnp.zeros((B, K), F32)
    codes = []
    for s in range(SLOTS):
        i = jnp.clip(list_ref[0, s] - r * 4, 0, 3)
        j = jnp.clip(list_ref[1, s] - c * 4, 0, 3)
        pair_of[s, 0] = i
        pair_of[s, 1] = j
        codes.append(jnp.where(s < count_ref[0, 0], i * 4 + j, -1))
    for pair in range(16):
        found = jnp.int32(SLOTS)
        for s in range(SLOTS):
            found = jnp.where(codes[s] == pair, s, found)
        slot_of[pair] = found

    def prepare(s):
        data_copy(s).wait()

        def part(h, carry):
            rows = pl.ds(pl.multiple_of(h * 64, 64), 64)
            level = stage[s, rows].astype(F32)
            bias[s, rows] = -jnp.log(jnp.maximum(level, 1.0)).astype(BF16)
            weight[s, rows] = jnp.where(level > 0.0, 0.1 + 0.25 * jnp.sqrt(level), 0.0).astype(BF16)
            return carry

        lax.fori_loop(0, B // 64, part, 0)

    loop(0, 3, prepare)
    relay_own(0)
    prepare(3)
    relay_other(0)
    pass_on(0)
    pass_back(0)
    prepare(4)
    hand_near(0)
    loop(5, SLOTS, prepare)
    hand_far(0)
    gather_end(0)
    arrange(0)

    lane = lax.broadcasted_iota(jnp.int32, (ROWS, 128), 1)
    mine = lane == lax.broadcasted_iota(jnp.int32, (ROWS, 128), 0)

    def pick(n):
        source = lax.rem(z - offset(n) + 2 * NZ, NZ)
        for side in range(2):
            for k in range(2):
                rows = pl.ds(pl.multiple_of(source * 64 + side * 32 + k * ROWS, ROWS), ROWS)
                margins = row_got_panel[0, k, n, side, 4].astype(F32)
                for i in range(4):
                    line = jnp.broadcast_to(margins[i : i + 1, 0:128], (ROWS, 128))
                    picked[i, rows, :] = jnp.where(mine, line, 0.0).astype(BF16)

    loop(0, 8, pick)
    ones = jnp.ones((128, 128), BF16)
    for i in range(4):
        marg_left[i] = jnp.dot(picked[i], ones, preferred_element_type=F32)
    for g in range(NROW // 2):
        low = col_panel[0, 2 * g, 16].astype(F32)[:, 0:128]
        high = col_panel[0, 2 * g + 1, 16].astype(F32)[:, 0:128]
        marg_right[:, g * 128 : (g + 1) * 128] = jnp.where(lane < COLS, low, pltpu.roll(high, COLS, 1))

    def tiles(p):
        def tile(s):
            i, j = pair_of[s, 0], pair_of[s, 1]
            col_piece = col_panel[p, :, pl.ds(4 * j, 4)].reshape(B, K)
            row_piece = row_panel[i]
            scores = lax.dot_general(row_piece, col_piece, (((1,), (1,)), ((), ())), preferred_element_type=F32)
            if p == 0:
                left = jnp.concatenate([marg_left[i]] * (B // 128), axis=1)
                shift = (bias[s].astype(F32) + marg_right[pl.ds(j, 1), :] + left).astype(BF16)
                bias[s] = shift
            else:
                shift = bias[s]
            diff = scores.astype(BF16) + shift
            scale = weight[s]
            signal = jnp.where(scale > 0, scale * diff, 0.5 * jnp.tanh(0.5 * diff) + 0.5).astype(BF16)
            signals[s] = signal
            col_term[s] = lax.dot_general(signal, row_piece, (((0,), (0,)), ((), ())), preferred_element_type=F32)

        for s in range(SLOTS):
            tile(s)

    def row_terms(p):
        for s in range(SLOTS):
            col_piece = col_panel[p, :, pl.ds(4 * pair_of[s, 1], 4)].reshape(B, K)
            row_term[s] = jnp.dot(signals[s], col_piece, preferred_element_type=F32)

    far, near = pl.ds(NEAR, 8 - NEAR), pl.ds(0, NEAR)

    def sibling_send(p, part):
        slots = near if part == 0 else far
        return copy(
            row_send.at[1 - core, slots], row_half.at[p, slots], sib_s.at[p, part], sib_r.at[p, part], sibling
        )

    def far_sends(p):
        return [
            copy(row_sum.at[7, 0], row_last.at[p, 0], rg_s.at[p, 12], rg_r.at[p, 12], at_z(2)),
            copy(row_sum.at[7, 1], row_last.at[p, 1], rg_s.at[p, 13], rg_r.at[p, 13], at_z(-2)),
            copy(row_sum.at[5], row_far.at[p, 0], rg_s.at[p, 10], rg_r.at[p, 10], at_z(1)),
            copy(row_sum.at[6], row_far.at[p, 1], rg_s.at[p, 11], rg_r.at[p, 11], at_z(-1)),
        ]

    def near_sends(p, slots):
        out = []
        for other in (1, 0):
            for m in slots:
                if m == 0 and other == 0:
                    continue
                sem = m * 2 + other
                side = xh if other == 0 else 1 - xh
                out.append(
                    copy(
                        row_sum.at[m, side], row_got.at[p, sem], rg_s.at[p, sem], rg_r.at[p, sem],
                        at_z(offset(m), other),
                    )
                )
        return out

    def cross_send(p, q):
        t = (1 - xl) * NY + lax.rem(y + q, NY)
        device = at_x() if q == 2 else at_y(q)
        return copy(col_send.at[t], col_cross.at[p, q], cg_s.at[p, NY + q], cg_r.at[p, NY + q], device)

    def straight_send(p, q):
        t = xl * NY + lax.rem(y + q, NY)
        return copy(col_send.at[t], col_got.at[p, q], cg_s.at[p, q], cg_r.at[p, q], at_y(q))

    def across_send(p):
        return copy(col_send.at[across], col_got.at[p, 0], cg_s.at[p, NY], cg_r.at[p, NY], at_x())

    def row_part(m):
        dest = lax.rem(z + offset(m) + NZ, NZ)
        for side in range(2):
            for k in range(2):
                rows = pl.ds(pl.multiple_of(dest * 64 + side * 32 + k * ROWS, ROWS), ROWS)
                for i in range(4):
                    found = [row_term[slot_of[i * 4 + j], rows, :] for j in range(4)]
                    row_send[k, m, side, i] = ((found[0] + found[1]) + (found[2] + found[3])).astype(BF16)

    def col_part(t):
        for part in range(2):
            rows = pl.ds(pl.multiple_of(t * COLS + part * 32, 32), 32)
            for j in range(4):
                found = [col_term[slot_of[i * 4 + j], rows, :] for i in range(4)]
                col_send[t, j, part * 32 : part * 32 + 32] = (
                    (found[0] + found[1]) + (found[2] + found[3])
                ).astype(BF16)

    def add(p, m):
        for side in range(2):
            row_sum[m, side] = (
                row_send[core, m, side].astype(F32) + row_half[p, m, side].astype(F32)
            ).astype(BF16)

    def col_add(p, t, crossed):
        for j in range(4):
            total = col_send[t, j].astype(F32)
            for q in crossed:
                total = total + col_cross[p, q, j].astype(F32)
            col_send[t, j] = total.astype(BF16)

    def scatter(p):
        col_part((1 - xl) * NY + lax.rem(y + 2, NY))
        cross_send(p, 2).start()
        for q in (1, 3):
            col_part((1 - xl) * NY + lax.rem(y + q, NY))
            cross_send(p, q).start()
        row_terms(p)
        loop(NEAR, 8, row_part)
        sibling_send(p, 1).start()
        loop(0, NEAR, row_part)
        sibling_send(p, 0).start()
        sibling_send(p, 1).wait_recv()
        for m in range(NEAR, 8):
            add(p, m)
        for send in far_sends(p):
            send.start()
        col_part(xl * NY + lax.rem(y + 2, NY))
        col_part(across)
        sibling_send(p, 0).wait_recv()
        for m in range(NEAR):
            add(p, m)
        for send in near_sends(p, (1, 2, 0)):
            send.start()
        cross_send(p, 2).wait_recv()
        col_add(p, xl * NY + lax.rem(y + 2, NY), (2,))
        straight_send(p, 2).start()
        for q in (1, 3):
            col_part(xl * NY + lax.rem(y + q, NY))
        col_part(r)
        last_0, last_1, far_0, far_1 = far_sends(p)
        for m, e, sends in ((3, 0, (far_0, last_0)), (4, 1, (far_1, last_1))):
            for send in sends:
                send.wait_recv()
            for side in range(2):
                total = row_sum[m, side].astype(F32) + row_far[p, e, side].astype(F32)
                if side == e:
                    total = total + row_last[p, e].astype(F32)
                row_sum[m, side] = total.astype(BF16)
            for send in near_sends(p, (m,)):
                send.start()
        for q in (1, 3):
            cross_send(p, q).wait_recv()
        col_add(p, across, (1, 3))
        across_send(p).start()
        for q in (1, 3):
            straight_send(p, q).start()

    def row_update(p):
        for send in near_sends(p, range(NEAR)):
            send.wait_recv()
        total = row_sum[0, xh].astype(F32)
        for sem in range(1, 2 * NEAR):
            total = total + row_got[p, sem].astype(F32)
        row_now[...] = row_now[...] - 0.0004 * total

    def col_update(p):
        for q in ys:
            straight_send(p, q).wait_recv()
        across_send(p).wait_recv()
        for j in range(4):
            total = col_send[r, j].astype(F32)
            for q in range(NY):
                total = total + col_got[p, q, j].astype(F32)
            col_now[j] = col_now[j] - 0.0004 * total

    def scatter_sent(p):
        for q in ys:
            cross_send(p, q).wait_send()
            straight_send(p, q).wait_send()
        across_send(p).wait_send()
        for send in far_sends(p) + near_sends(p, range(NEAR)):
            send.wait_send()
        for part in range(2):
            sibling_send(p, part).wait_send()

    tiles(0)
    scatter(0)
    row_update(0)
    row_round(1)
    row_gather_send(1)
    col_update(0)
    col_round(1)
    col_gather_send(1)
    scatter_sent(0)
    relay_own(1)
    relay_other(1)
    pass_on(1)
    pass_back(1)
    hand_near(1)
    hand_far(1)
    gather_end(1)
    arrange(1)
    tiles(1)
    scatter(1)
    row_update(1)
    row_back = pltpu.make_async_copy(row_now, row_out, out_sem.at[0])
    row_back.start()
    col_update(1)
    col_back = pltpu.make_async_copy(col_now, col_out, out_sem.at[1])
    col_back.start()
    scatter_sent(1)
    gather_sent(0)
    gather_sent(1)
    row_back.wait()
    col_back.wait()


def finish(row_ref, col_ref, row_out, col_out, row_now, col_now, sem):
    ways = [(row_ref, row_now, row_out), (col_ref, col_now, col_out)]
    coming = [pltpu.make_async_copy(src, now, sem.at[k]) for k, (src, now, _) in enumerate(ways)]
    going = [pltpu.make_async_copy(now, dst, sem.at[2 + k]) for k, (_, now, dst) in enumerate(ways)]
    for copy in coming:
        copy.start()
    for k in range(2):
        coming[k].wait()
        going[k].start()
    for copy in going:
        copy.wait()


def shards(row_emb, col_emb, row_marg, col_marg, tile_list, tile_count, tile_data):
    vmem = pl.BlockSpec(memory_space=pltpu.VMEM)
    smem = pl.BlockSpec(memory_space=pltpu.SMEM)
    dma = pltpu.SemaphoreType.DMA
    where = pl.BlockSpec(memory_space=pl.ANY)
    news = pl.pallas_call(
        kernel,
        out_shape=(
            jax.ShapeDtypeStruct(row_emb.shape, F32),
            jax.ShapeDtypeStruct(col_emb.shape, F32),
        ),
        in_specs=[smem, smem, where, where, vmem, vmem, where],
        out_specs=(where, where),
        scratch_shapes=[
            pltpu.VMEM(row_emb.shape, F32),
            pltpu.VMEM(col_emb.shape, F32),
            pltpu.VMEM((2, 2, 8, 2, 5, ROWS, K), BF16),
            pltpu.VMEM((2, NROW, 17, 16, K), BF16),
            pltpu.VMEM((4, B, K), BF16),
            pltpu.VMEM((2, 16, K), F32),
            pltpu.VMEM((4, B, 128), BF16),
            pltpu.VMEM((4, B, 128), F32),
            pltpu.VMEM((16, B), F32),
            pltpu.VMEM((SLOTS, B, B), BF16),
            pltpu.VMEM((SLOTS, B, B), BF16),
            pltpu.VMEM((SLOTS, B, B), jnp.int32),
            pltpu.VMEM((SLOTS, B, B), BF16),
            pltpu.VMEM((SLOTS + 1, B, K), F32),
            pltpu.VMEM((SLOTS + 1, B, K), F32),
            pltpu.VMEM((2, 8, 2, 4, ROWS, K), BF16),
            pltpu.VMEM((2, 8, 2, 4, ROWS, K), BF16),
            pltpu.VMEM((8, 2, 4, ROWS, K), BF16),
            pltpu.VMEM((2, 2, 2, 4, ROWS, K), BF16),
            pltpu.VMEM((2, 2, 4, ROWS, K), BF16),
            pltpu.VMEM((2, 2 * NEAR, 4, ROWS, K), BF16),
            pltpu.VMEM((NROW, 4, COLS, K), BF16),
            pltpu.VMEM((2, NY, 4, COLS, K), BF16),
            pltpu.VMEM((2, NY, 4, COLS, K), BF16),
            pltpu.SMEM((16,), jnp.int32),
            pltpu.SMEM((SLOTS, 2), jnp.int32),
            dma((SLOTS,)), dma((2,)), dma((2,)),
            dma((2, 16)), dma((2, 16)), dma((2, 4)), dma((2, 4)), dma((2, NROW)), dma((2, NROW)),
            dma((2, 2)), dma((2, 2)), dma((2, 14)), dma((2, 14)), dma((2, NROW)), dma((2, NROW)),
        ],
        name="swivel",
        compiler_params=pltpu.CompilerParams(
            collective_id=0, has_side_effects=True, vmem_limit_bytes=60 * 2**20
        ),
        cost_estimate=pl.CostEstimate(flops=6_400_000_000, bytes_accessed=9_000_000, transcendentals=8_000_000),
    )(tile_count, tile_list[0, 0].T, row_emb, col_emb, row_marg, col_marg, tile_data)
    return pl.pallas_call(
        finish,
        out_shape=tuple(jax.ShapeDtypeStruct(new.shape, F32) for new in news),
        in_specs=[where, where],
        out_specs=(where, where),
        scratch_shapes=[pltpu.VMEM(new.shape, F32) for new in news] + [dma((4,))],
        name="finish",
    )(*news)


def solution(mesh):
    placed = (
        P("row", "col", None),
        P("col", "row", None),
        P("row", "col"),
        P("col", "row"),
        P("row", "col", None, None),
        P("row", "col"),
        P("row", "col", None, None, None),
    )
    return jax.shard_map(
        shards,
        mesh=mesh,
        in_specs=placed,
        out_specs=(P("row", "col", None), P("col", "row", None)),
        check_vma=False,
    )
```
